256 devices in a mesh: tower: 2 (over x_lo), dp: 16 (over x_hi, y, core), mp: 8 (over z).
Axes of the slice: x: 4 (x_hi: 2, x_lo: 2; x = x_hi * 2 + x_lo), y: 4, z: 8, core: 2. Of those that a mesh axis runs over, the one named last changes fastest.
Arguments:
- image_feats: bfloat16 [12288, 1664], P('dp', 'mp'), may hold values from -4 to 4
- text_feats: bfloat16 [12288, 1280], P('dp', 'mp'), may hold values from -4 to 4
- labels: int32 [12288], replicated, may hold values from 0 to 12287, each once
- logit_scale: float32 [1], replicated, may hold values from 20 to 100
- params: float32 [2, 8, 208, 1280], P('tower', 'mp'), may hold values from -0.07354355 to 0.07354355
- momentum: float32 [2, 8, 208, 1280], P('tower', 'mp'), may hold values from -6 to 6
- variance: float32 [2, 8, 208, 1280], P('tower', 'mp'), may hold values from 0.25 to 4
- worker_error: float32 [2, 16, 8, 208, 1280], P('tower', 'dp', 'mp'), may hold values from -4 to 4
- server_error: float32 [2, 8, 208, 1280], P('tower', 'mp', 'dp'), may hold values from -4 to 4
Outputs:
- weights_new: float32 [2, 8, 208, 1280], P('tower', 'mp')
- momentum_new: float32 [2, 8, 208, 1280], P('tower', 'mp')
- worker_new: float32 [2, 16, 8, 208, 1280], P('tower', 'dp', 'mp')
- server_new: float32 [2, 8, 208, 1280], P('tower', 'mp', 'dp')
The draws below stay inside these ranges and needn't reach their ends.
Inputs may be any that keep to these rules, and one draw needn't show every extreme that they name: `labels`: each number occurs once.
All inputs are finite; a program needn't handle non-finite values. Where the reference program divides by a largest or mean magnitude, that divisor is 1e-20 or more.
Results may differ from the reference program's by a relative error of at most 0.01155.
Values may be sent and summed in bfloat16 or wider, within the bound.
No kernel may reach another device: no remote copies, remote signals or barrier semaphores. Data moves between devices by JAX's collectives and lax.ppermute only.
A program may use at most 128 MiB of HBM per device.

```python
import math
import jax
import jax.numpy as jnp
from jax import lax

WI = 1664
WT = 1280
E = 1280
BATCH = 12288
S = 208
RB = 13
N_DP = 16
N_MP = 8


def draw_image_feats(key, part):
    key = jax.random.fold_in(key, 3)
    result = jnp.clip(jax.random.normal(key, (BATCH, WI), jnp.float32), -4.0, 4.0)
    return result.astype(jnp.bfloat16)


def draw_text_feats(key, part):
    key = jax.random.fold_in(key, 4)
    result = jnp.clip(jax.random.normal(key, (BATCH, WT), jnp.float32), -4.0, 4.0)
    return result.astype(jnp.bfloat16)


def draw_params(key, part):
    key = jax.random.fold_in(key, 5)
    base = jnp.clip(jax.random.normal(key, (2, N_MP, WI // N_MP, E), jnp.float32), -3.0, 3.0) * WI ** (-0.5)
    return base


def draw_logit_scale(key, part):
    key = jax.random.fold_in(key, 11)
    value = jnp.exp(jax.random.uniform(key, (1,), jnp.float32, math.log(20.0), math.log(100.0)))
    return value


def levels(key, extent, shards, least, largest):
    level = 1.0
    for dim, shards_of in shards:
        steps = jax.random.uniform(jax.random.fold_in(jax.random.fold_in(key, 6), dim), (shards_of,), jnp.float32, least / len(shards), largest / len(shards))
        level = level * jnp.repeat(jnp.exp(steps), extent[dim] // shards_of).reshape((-1,) + (1,) * (len(extent) - 1 - dim))
    return level


def scatter_about(key, extent, scale, most, cuts=(), held_as=jnp.bfloat16):
    gain = levels(key, extent, cuts, -0.22, 0.18) if cuts else 1.0
    values = jax.random.normal(key, extent, jnp.float32) * scale * gain
    return jnp.minimum(jnp.maximum(values, -most), most).astype(held_as)


def setup_inputs(seed: int = 0) -> dict:
    key_list = jax.random.split(jax.random.key(seed), 10)
    return {
        "image_feats": draw_image_feats(jax.random.fold_in(key_list[9], 71), 0),
        "text_feats": draw_text_feats(jax.random.fold_in(key_list[9], 71), 0),
        "labels": jax.random.permutation(key_list[2], BATCH).astype(jnp.int32),
        "logit_scale": draw_logit_scale(jax.random.fold_in(key_list[9], 71), 0),
        "params": draw_params(jax.random.fold_in(key_list[9], 71), 0),
        "momentum": scatter_about(key_list[5], (2, N_MP, S, E), 1.0, 6.0, ((0, 2), (1, 8)), jnp.float32),
        "variance": jnp.clip(jnp.exp(math.log(4.0) - 2.7725887 * jax.random.uniform(key_list[6], (2, N_MP, S, E), jnp.float32) ** levels(key_list[6], (2, N_MP, S, E), ((0, 2), (1, 8)), -0.2, 0.2)), 0.25, 4.0),
        "worker_error": scatter_about(key_list[7], (2, N_DP, N_MP, S, E), 0.3, 4.0, ((0, 2), (1, 16), (2, 8)), jnp.float32),
        "server_error": scatter_about(key_list[8], (2, N_MP, S, E), 0.3, 4.0, ((0, 2), (1, 8), (2, 16)), jnp.float32),
    }


epsilon = 1e-06
beta_one = 0.9
step_size = 0.01
var_floor = 1e-08

def embed(feats, weight):
    raw = jnp.dot(feats, weight.astype(jnp.bfloat16), preferred_element_type=jnp.float32)
    norm = jnp.sqrt(lax.optimization_barrier(jnp.sum(raw * raw, axis=1, keepdims=True)) + epsilon)
    return (raw / norm, norm)

def direction(rows, cols, pair_of, scale):
    block_rows = math.gcd(BATCH, 1024)
    col_index = jnp.arange(BATCH, dtype=jnp.int32)

    def step(carry, index):
        start = (index * block_rows).astype(jnp.int32)
        block = lax.dynamic_slice_in_dim(rows, start, block_rows, 0)
        scores = scale * lax.dot_general(block, cols, (((1,), (1,)), ((), ())), preferred_element_type=jnp.float32)
        top = lax.optimization_barrier(jnp.max(scores, axis=1, keepdims=True))
        expd = jnp.exp(scores - top)
        probs = expd / lax.optimization_barrier(jnp.sum(expd, axis=1, keepdims=True))
        pairs = lax.dynamic_slice_in_dim(pair_of, start, block_rows, 0)
        target = (pairs[:, None] == col_index[None, :]).astype(jnp.float32)
        slope = ((probs - target) * (0.5 * scale)).astype(jnp.bfloat16)
        row_grad = jnp.dot(slope, cols, preferred_element_type=jnp.float32)
        carry = carry + lax.dot_general(slope, block, (((0,), (0,)), ((), ())), preferred_element_type=jnp.float32)
        return (carry, row_grad)
    col_grad, row_grads = lax.scan(step, jnp.zeros((BATCH, E), jnp.float32), jnp.arange(BATCH // block_rows, dtype=jnp.int32))
    return (row_grads.reshape(BATCH, E), col_grad)

def backnorm(demb, unit, norm):
    inner = lax.optimization_barrier(jnp.sum(unit * demb, axis=1, keepdims=True))
    return ((demb - unit * inner) / norm).astype(jnp.bfloat16)

def reference(image_feats, text_feats, labels, logit_scale, params, momentum, variance, worker_error, server_error):
    shard = WI // N_MP
    text_shard = WT // N_MP
    group_rows = BATCH // N_DP
    w_image = params[0].reshape(WI, E)
    w_text = params[1, :, :text_shard, :].reshape(WT, E)
    unit_img, norm_img = embed(image_feats, w_image)
    unit_txt, norm_txt = embed(text_feats, w_text)
    emb_img = unit_img.astype(jnp.bfloat16)
    emb_txt = unit_txt.astype(jnp.bfloat16)
    inverse = jnp.zeros((BATCH,), jnp.int32).at[labels].set(jnp.arange(BATCH, dtype=jnp.int32))
    scale = logit_scale[0]
    row_img, col_img = direction(emb_img, emb_txt, labels, scale)
    row_txt, col_txt = direction(emb_txt, emb_img, inverse, scale)
    lift_img = backnorm(row_img + col_txt, unit_img, norm_img)
    lift_txt = backnorm(row_txt + col_img, unit_txt, norm_txt)
    grad_img = jnp.einsum('rbw,rbe->rwe', image_feats.reshape(N_DP, group_rows, WI).astype(jnp.float32), lift_img.reshape(N_DP, group_rows, E).astype(jnp.float32))
    grad_txt = jnp.einsum('rbw,rbe->rwe', text_feats.reshape(N_DP, group_rows, WT).astype(jnp.float32), lift_txt.reshape(N_DP, group_rows, E).astype(jnp.float32))
    grad_img = grad_img.reshape(N_DP, N_MP, shard, E)
    grad_txt = jnp.pad(grad_txt.reshape(N_DP, N_MP, text_shard, E), ((0, 0), (0, 0), (0, shard - text_shard), (0, 0)))
    grads = jnp.stack([grad_img, grad_txt])
    moment = beta_one * momentum[:, None] + (1.0 - beta_one) * grads
    comp = moment + worker_error
    blocks = comp.reshape(2, N_DP, N_MP, N_DP, RB, E)
    scales = lax.optimization_barrier(jnp.mean(jnp.abs(blocks), axis=(4, 5)))
    scales = lax.optimization_barrier(scales.astype(jnp.bfloat16)).astype(jnp.float32)
    scales = scales[:, :, :, :, None, None]
    ramp = jnp.clip(blocks / (scales + epsilon), -1.0, 1.0).astype(jnp.bfloat16)
    restored = scales * ramp.astype(jnp.float32)
    worker_new = comp - restored.reshape(comp.shape)
    average = lax.optimization_barrier(jnp.mean(restored, axis=1)) + server_error.reshape(2, N_MP, N_DP, RB, E)
    server_scale = lax.optimization_barrier(jnp.mean(jnp.abs(average), axis=(3, 4)))
    server_scale = lax.optimization_barrier(server_scale.astype(jnp.bfloat16)).astype(jnp.float32)
    server_scale = server_scale[:, :, :, None, None]
    server_ramp = jnp.clip(average / (server_scale + epsilon), -1.0, 1.0).astype(jnp.bfloat16)
    settled = server_scale * server_ramp.astype(jnp.float32)
    server_new = (average - settled).reshape(2, N_MP, shard, E)
    momentum_new = settled.reshape(2, N_MP, shard, E)
    weights_new = params - step_size * momentum_new / (jnp.sqrt(variance) + var_floor)
    return (weights_new, momentum_new, worker_new, server_new)
```

```python
import jax
import jax.numpy as jnp
from jax import lax
from jax.experimental import pallas as pl
from jax.experimental.pallas import tpu as pltpu
from jax.sharding import Mesh, PartitionSpec as P

epsilon = 1e-06
beta_one = 0.9
step_size = 0.01
var_floor = 1e-08

high_shift = 24.0
low_shift = 68.0
low_cap = -30.0
tiny_sum = 8.75e-27


def core_lanes(core, line):
    return tuple(pl.ds(pl.multiple_of(c * line, 128), line) for c in (core, 1 - core))


def standing(row, count):
    return jnp.broadcast_to(row, (128, count)).T


def lying(column, count):
    return jnp.broadcast_to(column, (count, 128)).T[0:1]


def score_kernel(core_ref, scale_ref, near_ref, far_ref, cols_ref, scores_ref, row_ref, col_ref):
    step = pl.program_id(0)
    line = near_ref.shape[0]
    dims = (((1,), (1,)), ((), ()))
    near = lax.dot_general(near_ref[...], cols_ref[...], dims, preferred_element_type=jnp.float32)
    far = lax.dot_general(far_ref[...], cols_ref[...], dims, preferred_element_type=jnp.float32)

    @pl.when(step == 0)
    def _():
        scores_ref[:line] = near
        scores_ref[line:] = far

    @pl.when(step > 0)
    def _():
        scores_ref[:line] += near
        scores_ref[line:] += far

    @pl.when(step == pl.num_programs(0) - 1)
    def _():
        scale = scale_ref[0]
        count = scores_ref.shape[0]
        scores = scale * scores_ref[...]
        scores_ref[...] = scores
        near_lanes, far_lanes = core_lanes(core_ref[0], line)

        def put(which, row_sum, col_sum):
            row_ref[which : which + 1, near_lanes] = row_sum[:, :line]
            row_ref[which : which + 1, far_lanes] = row_sum[:, line:]
            for copy in range(col_ref.shape[0]):
                col_ref[copy, which : which + 1] = col_sum

        high = jnp.exp(scores - high_shift)
        row_high = lying(jnp.sum(high, axis=1, keepdims=True), count)
        col_high = jnp.sum(high, axis=0, keepdims=True)
        put(0, row_high, col_high)
        put(1, jnp.zeros_like(row_high), jnp.zeros_like(col_high))

        @pl.when(jnp.minimum(jnp.min(row_high), jnp.min(col_high)) < tiny_sum)
        def _():
            low = jnp.exp(jnp.minimum(scores_ref[...], low_cap) + low_shift)
            put(1, lying(jnp.sum(low, axis=1, keepdims=True), count),
                jnp.sum(low, axis=0, keepdims=True))


def scored(core, scale, near, far, cols, copies):
    line, width = near.shape
    count = cols.shape[0]
    wide = 256
    return pl.pallas_call(
        score_kernel,
        grid=(width // wide,),
        in_specs=[
            pl.BlockSpec(memory_space=pltpu.SMEM),
            pl.BlockSpec(memory_space=pltpu.SMEM),
            pl.BlockSpec((line, wide), lambda i: (0, i)),
            pl.BlockSpec((line, wide), lambda i: (0, i)),
            pl.BlockSpec((count, wide), lambda i: (0, i)),
        ],
        out_specs=[
            pl.BlockSpec((2 * line, count), lambda i: (0, 0)),
            pl.BlockSpec((2, 2 * line), lambda i: (0, 0)),
            pl.BlockSpec((copies, 2, count), lambda i: (0, 0, 0)),
        ],
        out_shape=[
            jax.ShapeDtypeStruct((2 * line, count), jnp.float32),
            jax.ShapeDtypeStruct((2, 2 * line), jnp.float32),
            jax.ShapeDtypeStruct((copies, 2, count), jnp.float32),
        ],
        compiler_params=pltpu.CompilerParams(vmem_limit_bytes=40 * 2**20),
        cost_estimate=pl.CostEstimate(
            flops=4 * line * count * width,
            bytes_accessed=2 * width * (2 * line + count) + 8 * line * count,
            transcendentals=2 * line * count,
        ),
    )(core, scale, near, far, cols)


def inverses(sums):
    is_high = sums[0:1] >= tiny_sum
    inverse = 1.0 / jnp.where(is_high, sums[0:1], sums[1:2])
    return jnp.where(is_high, inverse, 0.0), jnp.where(is_high, 0.0, inverse)


def slope_kernel(
    core_ref, scale_ref, scores_ref, row_sum_ref, row_target_ref, col_sum_ref, col_index_ref,
    near_ref, far_ref, cols_ref, near_out, far_out, col_out, slope_ref
):
    line = near_ref.shape[0]
    count = scores_ref.shape[0]

    @pl.when(pl.program_id(0) == 0)
    def _():
        near_lanes, far_lanes = core_lanes(core_ref[0], line)
        row_sums = jnp.concatenate([row_sum_ref[:, near_lanes], row_sum_ref[:, far_lanes]], 1)
        row_high, row_low = inverses(row_sums)
        col_high, col_low = inverses(col_sum_ref[...])
        target = standing(row_target_ref[...], count)[:, 0:1] == col_index_ref[...]
        aim = jnp.where(target, 2.0, 0.0)
        factor = 0.5 * scale_ref[0]
        high = jnp.exp(scores_ref[...] - high_shift)
        probs = high * (standing(row_high, count)[:, 0:1] + col_high)
        slope_ref[...] = ((probs - aim) * factor).astype(jnp.bfloat16)

        @pl.when(jnp.maximum(jnp.max(row_low), jnp.max(col_low)) > 0.0)
        def _():
            low = jnp.exp(jnp.minimum(scores_ref[...], low_cap) + low_shift)
            both = probs + low * (standing(row_low, count)[:, 0:1] + col_low)
            slope_ref[...] = ((both - aim) * factor).astype(jnp.bfloat16)

    cols = cols_ref[...]
    near_out[...] = jnp.dot(
        slope_ref[:line], cols, preferred_element_type=jnp.float32
    ).astype(jnp.bfloat16)
    far_out[...] = jnp.dot(
        slope_ref[line:], cols, preferred_element_type=jnp.float32
    ).astype(jnp.bfloat16)
    dims = (((0,), (0,)), ((), ()))
    col_out[...] = (
        lax.dot_general(slope_ref[:line], near_ref[...], dims, preferred_element_type=jnp.float32)
        + lax.dot_general(slope_ref[line:], far_ref[...], dims, preferred_element_type=jnp.float32)
    ).astype(jnp.bfloat16)


def sloped(core, scale, scores, row_sums, row_target, col_sums, col_index, near, far, cols):
    line, width = near.shape
    count = cols.shape[0]
    wide = 256
    whole = lambda a: pl.BlockSpec(a.shape, lambda i: (0, 0))
    part = lambda a: pl.BlockSpec((a.shape[0], wide), lambda i: (0, i))
    return pl.pallas_call(
        slope_kernel,
        grid=(width // wide,),
        in_specs=[pl.BlockSpec(memory_space=pltpu.SMEM)] * 2
        + [whole(a) for a in (scores, row_sums, row_target, col_sums, col_index)]
        + [part(a) for a in (near, far, cols)],
        out_specs=[part(near), part(far), part(cols)],
        out_shape=[jax.ShapeDtypeStruct(a.shape, jnp.bfloat16) for a in (near, far, cols)],
        scratch_shapes=[pltpu.VMEM(scores.shape, jnp.bfloat16)],
        compiler_params=pltpu.CompilerParams(vmem_limit_bytes=40 * 2**20),
        cost_estimate=pl.CostEstimate(
            flops=8 * line * count * width,
            bytes_accessed=4 * width * (2 * line + count) + 8 * line * count,
            transcendentals=2 * line * count,
        ),
    )(core, scale, scores, row_sums, row_target, col_sums, col_index, near, far, cols)

def join_kernel(mp_ref, *refs):
    pieces, out_ref = refs[:-1], refs[-1]
    count, rows = len(pieces), pieces[0].shape[0]
    for k, piece in enumerate(pieces):
        start = pl.multiple_of(lax.rem(mp_ref[0] + k, count) * rows, 16)
        out_ref[pl.ds(start, rows)] = piece[...]


def joined(mp, pieces):
    rows, width = pieces[0].shape
    return pl.pallas_call(
        join_kernel,
        in_specs=[pl.BlockSpec(memory_space=pltpu.SMEM)]
        + [pl.BlockSpec(memory_space=pltpu.VMEM)] * len(pieces),
        out_specs=pl.BlockSpec(memory_space=pltpu.VMEM),
        out_shape=jax.ShapeDtypeStruct((rows * len(pieces), width), pieces[0].dtype),
        compiler_params=pltpu.CompilerParams(vmem_limit_bytes=16 * 2**20),
        cost_estimate=pl.CostEstimate(
            flops=0, bytes_accessed=4 * rows * len(pieces) * width, transcendentals=0
        ),
    )(mp, *pieces)


def part_kernel(mp_ref, near_ref, far_ref, *outs):
    count, rows = len(outs), outs[0].shape[0]
    for k, out in enumerate(outs):
        start = pl.multiple_of(lax.rem(mp_ref[0] + k, count) * rows, 16)
        block = pl.ds(start, rows)
        total = near_ref[block].astype(jnp.float32) + far_ref[block].astype(jnp.float32)
        out[...] = total.astype(out.dtype)


def parted(mp, near, far, count):
    rows, width = near.shape[0] // count, near.shape[1]
    return pl.pallas_call(
        part_kernel,
        in_specs=[pl.BlockSpec(memory_space=pltpu.SMEM)]
        + [pl.BlockSpec(memory_space=pltpu.VMEM)] * 2,
        out_specs=[pl.BlockSpec(memory_space=pltpu.VMEM)] * count,
        out_shape=[jax.ShapeDtypeStruct((rows, width), near.dtype)] * count,
        compiler_params=pltpu.CompilerParams(vmem_limit_bytes=16 * 2**20),
        cost_estimate=pl.CostEstimate(
            flops=near.size, bytes_accessed=6 * near.size, transcendentals=0
        ),
    )(mp, near, far)


def owner_rows(mp, tower, k, part, owners, half):
    which = tower if part else 1 - tower
    start = (lax.rem(mp + k, owners) * 2 + which) * half
    return pl.ds(pl.multiple_of(start, 16), half)


def project_kernel(mp_ref, tower_ref, image_ref, text_ref, weight_ref, *refs):
    outs, (raw_ref,) = refs[:-1], refs[-1:]
    half, width = outs[0].shape
    wide = 256
    dims = (((0,), (0,)), ((), ()))

    def fill(feats_ref):
        count = feats_ref.shape[0]
        for start in range(0, width, wide):
            part = slice(start, start + wide)
            raw_ref[:, part] = lax.dot_general(
                feats_ref[...],
                weight_ref[:count, part].astype(jnp.bfloat16),
                dims,
                preferred_element_type=jnp.float32,
            ).astype(jnp.bfloat16)

    @pl.when(tower_ref[0] == 0)
    def _():
        fill(image_ref)

    @pl.when(tower_ref[0] != 0)
    def _():
        fill(text_ref)

    owners = len(outs) // 2
    for n, out in enumerate(outs):
        out[...] = raw_ref[owner_rows(mp_ref[0], tower_ref[0], n // 2, n % 2, owners, half)]


def projected(mp, tower, image, text, weight, owners):
    rows, width = image.shape[1], weight.shape[1]
    half = rows // (2 * owners)
    return pl.pallas_call(
        project_kernel,
        in_specs=[pl.BlockSpec(memory_space=pltpu.SMEM)] * 2
        + [pl.BlockSpec(memory_space=pltpu.VMEM)] * 3,
        out_specs=[pl.BlockSpec(memory_space=pltpu.VMEM)] * (2 * owners),
        out_shape=[jax.ShapeDtypeStruct((half, width), jnp.bfloat16)] * (2 * owners),
        scratch_shapes=[pltpu.VMEM((rows, width), jnp.bfloat16)],
        compiler_params=pltpu.CompilerParams(vmem_limit_bytes=32 * 2**20),
        cost_estimate=pl.CostEstimate(
            flops=2 * rows * weight.size, bytes_accessed=4 * rows * width, transcendentals=0
        ),
    )(mp, tower, image, text, weight)


def grad_kernel(mp_ref, tower_ref, core_ref, image_ref, text_ref, carried_ref, *refs):
    pieces = refs[:-5]
    worker_ref, mine_ref, other_ref, lift_ref, rest_ref = refs[-5:]
    half = pieces[0].shape[0]
    shard_rows, width = worker_ref.shape
    blocks = 2 * mine_ref.shape[0]
    row_block = shard_rows // blocks
    owners = len(pieces) // 2
    for n, piece in enumerate(pieces):
        lift_ref[owner_rows(mp_ref[0], tower_ref[0], n // 2, n % 2, owners, half)] = piece[...]
    wide = 256

    def fill(feats_ref):
        count = feats_ref.shape[0]
        for start in range(0, width, wide):
            part = slice(start, start + wide)
            grad = jnp.dot(
                feats_ref[...], lift_ref[:, part], preferred_element_type=jnp.float32
            )
            worker_ref[:count, part] = (1.0 - beta_one) * grad + carried_ref[:count, part]
        if count < shard_rows:
            worker_ref[count:] = carried_ref[count:]

    @pl.when(tower_ref[0] == 0)
    def _():
        fill(image_ref)

    @pl.when(tower_ref[0] != 0)
    def _():
        fill(text_ref)

    comp = worker_ref[...]
    row_abs = jnp.sum(jnp.abs(comp), axis=1, keepdims=True)
    row = lax.broadcasted_iota(jnp.int32, (shard_rows, 1), 0)
    scale = jnp.zeros((shard_rows, 1), jnp.float32)
    for b in range(blocks):
        inside = (row >= b * row_block) & (row < (b + 1) * row_block)
        total = jnp.sum(jnp.where(inside, row_abs, 0.0), axis=0, keepdims=True)
        scale = jnp.where(inside, total / (row_block * width), scale)
    scale = jnp.broadcast_to(scale, (shard_rows, 128)).astype(jnp.bfloat16).astype(jnp.float32)
    scale = scale[:, 0:1]
    ramp = jnp.clip(comp / (scale + epsilon), -1.0, 1.0).astype(jnp.bfloat16)
    restored = scale * ramp.astype(jnp.float32)
    worker_ref[...] = comp - restored
    tall = mine_ref.shape[1]
    rest_ref[:shard_rows] = restored
    rest_ref[shard_rows:] = jnp.zeros((rest_ref.shape[0] - shard_rows, width), jnp.float32)
    valid = lax.broadcasted_iota(jnp.int32, (tall, 1), 0) < row_block
    even = core_ref[0] == 0
    for b in range(blocks // 2):
        first = 2 * b * row_block
        one = jnp.where(valid, rest_ref[first : first + tall], 0.0)
        two = jnp.where(valid, rest_ref[first + row_block : first + row_block + tall], 0.0)
        mine_ref[b] = jnp.where(even, one, two).astype(jnp.bfloat16)
        other_ref[b] = jnp.where(even, two, one).astype(jnp.bfloat16)


def graded(mp, tower, core, image, text, carried, pieces, blocks):
    shard_rows, width = carried.shape
    rows = image.shape[1]
    sent = jax.ShapeDtypeStruct((blocks // 2, 16, width), jnp.bfloat16)
    return pl.pallas_call(
        grad_kernel,
        in_specs=[pl.BlockSpec(memory_space=pltpu.SMEM)] * 3
        + [pl.BlockSpec(memory_space=pltpu.VMEM)] * (3 + len(pieces)),
        out_specs=[pl.BlockSpec(memory_space=pltpu.VMEM)] * 3,
        out_shape=[jax.ShapeDtypeStruct(carried.shape, jnp.float32), sent, sent],
        scratch_shapes=[
            pltpu.VMEM((rows, width), jnp.bfloat16),
            pltpu.VMEM((shard_rows + 16, width), jnp.float32),
        ],
        compiler_params=pltpu.CompilerParams(vmem_limit_bytes=32 * 2**20),
        cost_estimate=pl.CostEstimate(
            flops=2 * rows * shard_rows * width,
            bytes_accessed=2 * rows * width + 12 * shard_rows * width,
            transcendentals=0,
        ),
    )(mp, tower, core, image, text, carried, *pieces)


def server_kernel(got_ref, error_ref, new_ref, reply_ref, rest_ref):
    row_block, width = error_ref.shape
    halves = got_ref.shape[0]
    total = got_ref[0].astype(jnp.float32)
    for b in range(1, halves):
        total = total + got_ref[b].astype(jnp.float32)
    rest_ref[...] = total
    average = rest_ref[:row_block] / (2 * halves) + error_ref[...]
    scale = jnp.sum(jnp.sum(jnp.abs(average), axis=1, keepdims=True), axis=0, keepdims=True)
    scale = jnp.broadcast_to(scale / (row_block * width), (16, width))
    scale = scale.astype(jnp.bfloat16).astype(jnp.float32)
    ramp = jnp.clip(average / (scale[:row_block] + epsilon), -1.0, 1.0).astype(jnp.bfloat16)
    ramp = ramp.astype(jnp.float32)
    new_ref[...] = average - scale[:row_block] * ramp
    rest_ref[...] = scale
    rest_ref[:row_block] = ramp
    reply = rest_ref[...].astype(jnp.bfloat16)
    for b in range(halves):
        reply_ref[b] = reply


def served(got, error):
    return pl.pallas_call(
        server_kernel,
        in_specs=[pl.BlockSpec(memory_space=pltpu.VMEM)] * 2,
        out_specs=[pl.BlockSpec(memory_space=pltpu.VMEM)] * 2,
        out_shape=[
            jax.ShapeDtypeStruct(error.shape, jnp.float32),
            jax.ShapeDtypeStruct(got.shape, jnp.bfloat16),
        ],
        scratch_shapes=[pltpu.VMEM(got.shape[1:], jnp.float32)],
        compiler_params=pltpu.CompilerParams(vmem_limit_bytes=16 * 2**20),
        cost_estimate=pl.CostEstimate(
            flops=got.size, bytes_accessed=4 * got.size, transcendentals=0
        ),
    )(got, error)


def update_kernel(core_ref, near_ref, far_ref, params_ref, rate_ref, weights_ref, moment_ref):
    halves = near_ref.shape[0]
    row_block = params_ref.shape[0] // (2 * halves)
    even = core_ref[0] == 0
    for b in range(halves):
        near = near_ref[b].astype(jnp.float32)
        far = far_ref[b].astype(jnp.float32)
        for c, block in enumerate((jnp.where(even, near, far), jnp.where(even, far, near))):
            first = (2 * b + c) * row_block
            rows = slice(first, first + row_block)
            moment_ref[rows] = block[:row_block] * block[row_block : row_block + 1]
    weights_ref[...] = params_ref[...] - rate_ref[...] * moment_ref[...]


def updated(core, near, far, params, rate):
    shape = jax.ShapeDtypeStruct(params.shape, jnp.float32)
    return pl.pallas_call(
        update_kernel,
        in_specs=[pl.BlockSpec(memory_space=pltpu.SMEM)]
        + [pl.BlockSpec(memory_space=pltpu.VMEM)] * 4,
        out_specs=[pl.BlockSpec(memory_space=pltpu.VMEM)] * 2,
        out_shape=[shape, shape],
        compiler_params=pltpu.CompilerParams(vmem_limit_bytes=32 * 2**20),
        cost_estimate=pl.CostEstimate(
            flops=3 * params.size, bytes_accessed=20 * params.size, transcendentals=0
        ),
    )(core, near, far, params, rate)


XY = ("tower", "xh", "y")
X2 = ("xh", "y")
DP = ("xh", "y", "core")


def shifted(block, axis, count, shift):
    return lax.ppermute(block, axis, [((i + shift) % count, i) for i in range(count)])


def crossed(block, axis, count, flip):
    return lax.ppermute(block, axis, [(i, i ^ flip) for i in range(count)])


def from_each(blocks, axis):
    return lax.all_to_all(blocks, axis, split_axis=0, concat_axis=0, tiled=True)


def ring_sum(term, axis, count):
    wide, narrow = jnp.float32, jnp.bfloat16
    ahead = term(count // 2)
    for k in range(count // 2 - 1, -1, -1):
        ahead = shifted(ahead.astype(narrow), axis, count, -1).astype(wide) + term(k)
    behind = term(count // 2 + 1)
    for k in range(count // 2 + 2, count):
        behind = shifted(behind.astype(narrow), axis, count, 1).astype(wide) + term(k)
    return ahead + shifted(behind.astype(narrow), axis, count, 1).astype(wide)


def body(
    image_feats,
    text_feats,
    labels,
    logit_scale,
    params,
    momentum,
    variance,
    worker_error,
    server_error,
):
    tower = lax.axis_index("tower")
    x_hi = lax.axis_index("xh")
    y = lax.axis_index("y")
    core = lax.axis_index("core")
    mp = lax.axis_index("mp")
    mp_count = lax.axis_size("mp")
    dp_count = lax.axis_size(DP)
    xy_count = lax.axis_size(XY)
    group_rows = image_feats.shape[0]
    per_dev = group_rows // mp_count
    half = per_dev // 2
    line = mp_count * half
    text_width = text_feats.shape[1]
    shard_rows = params.shape[2]
    width = params.shape[3]
    row_block = shard_rows // dp_count
    is_image = tower == 0
    f32, bf16 = jnp.float32, jnp.bfloat16

    mp_at, tower_at, core_at = (i.astype(jnp.int32).reshape(1) for i in (mp, tower, core))
    image, text = image_feats.T, text_feats.T
    partial = projected(mp_at, tower_at, image, text, params[0, 0], mp_count)

    def embedded(part):
        raw = ring_sum(lambda k: partial[2 * k + part].astype(f32), "mp", mp_count)
        norm = jnp.sqrt(jnp.sum(raw * raw, axis=1, keepdims=True) + epsilon)
        unit = raw / norm
        return unit, norm, unit.astype(bf16)

    out_unit, out_norm, out_emb = embedded(0)
    swapped = crossed(out_emb, "tower", 2, 1)
    kept_unit, kept_norm, kept = embedded(1)
    image_own = jnp.where(is_image, kept, swapped)
    text_own = jnp.where(is_image, swapped, kept)

    cols = from_each(
        jnp.broadcast_to(text_own[None], (xy_count, half, width)), XY
    ).reshape(xy_count * half, width)
    near = joined(
        mp_at, [image_own] + [shifted(image_own, "mp", mp_count, k) for k in range(1, mp_count)]
    )
    far = crossed(near, "core", 2, 1)

    place = (x_hi * 4 + y) * 2
    label_blocks = labels.reshape(dp_count, mp_count, 2, half)

    def line_labels(which_core):
        one = lax.dynamic_index_in_dim(label_blocks, place + which_core, 0, False)
        return lax.dynamic_index_in_dim(one, tower, 1, False).reshape(1, -1)

    row_target = jnp.concatenate([line_labels(core), line_labels(1 - core)], 1).astype(f32)
    owner = jnp.arange(xy_count, dtype=jnp.int32)
    col_index = (
        ((owner % 8 * 2 + core) * group_rows + mp * per_dev + owner // 8 * half)[:, None]
        + jnp.arange(half, dtype=jnp.int32)[None, :]
    ).reshape(1, -1).astype(f32)
    row_target, col_index = lax.optimization_barrier((row_target, col_index))

    scores, row_sums, col_sums = scored(core_at, logit_scale, near, far, cols, xy_count)

    col_sums = jnp.sum(from_each(col_sums, XY), axis=0)
    row_sums = lax.psum(row_sums + crossed(row_sums, "core", 2, 1), "mp")

    near_part, far_part, col_part = sloped(
        core_at, logit_scale, scores, row_sums, row_target, col_sums, col_index, near, far, cols
    )

    passed = crossed(far_part, "core", 2, 1)
    text_grad = jnp.sum(
        from_each(col_part.reshape(xy_count, half, width), XY).astype(f32), axis=0
    )
    sent = parted(mp_at, near_part, passed, mp_count)
    image_grad = sent[0].astype(f32)
    for k in (4, 3, 5, 2, 6, 1, 7):
        image_grad = image_grad + shifted(sent[k], "mp", mp_count, -k).astype(f32)

    kept_grad = jnp.where(is_image, image_grad, text_grad)
    out_grad = crossed(
        jnp.where(is_image, text_grad, image_grad).astype(bf16), "tower", 2, 1
    ).astype(f32)

    def lifted(unit, norm, grad):
        inner = jnp.sum(unit * grad, axis=1, keepdims=True)
        return ((grad - unit * inner) / norm).astype(bf16)

    pieces = {}
    kept_lift = lifted(kept_unit, kept_norm, kept_grad)
    out_lift = lifted(out_unit, out_norm, out_grad)
    for part, lift in ((1, kept_lift), (0, out_lift)):
        ahead = behind = lift
        pieces[0, part] = lift
        for step in range(1, mp_count // 2 + 1):
            behind = shifted(behind, "mp", mp_count, -1)
            pieces[mp_count - step, part] = behind
            if step < mp_count // 2:
                ahead = shifted(ahead, "mp", mp_count, 1)
                pieces[step, part] = ahead
    carried = beta_one * momentum[0, 0] + worker_error[0, 0, 0]
    rate = step_size / (jnp.sqrt(variance[0, 0]) + var_floor)
    carried, rate = lax.optimization_barrier((carried, rate))
    worker_new, mine, other = graded(
        mp_at,
        tower_at,
        core_at,
        image,
        text,
        carried,
        [pieces[k, part] for k in range(mp_count) for part in range(2)],
        dp_count,
    )

    pair = mine.astype(f32) + crossed(other, "core", 2, 1).astype(f32)
    server_new, reply = served(from_each(pair.astype(bf16), X2), server_error[0, 0])
    near_reply = from_each(reply, X2)
    far_reply = crossed(near_reply, "core", 2, 1)
    weights_new, momentum_new = updated(core_at, near_reply, far_reply, params[0, 0], rate)
    return (
        weights_new[None, None],
        momentum_new[None, None],
        worker_new[None, None, None],
        server_new[None, None],
    )


def solution(mesh):
    fine = Mesh(mesh.devices.reshape(2, 2, 4, 2, 8), ("tower", "xh", "y", "core", "mp"))
    return jax.shard_map(
        body,
        mesh=fine,
        in_specs=(
            P(DP, "mp"),
            P(DP, "mp"),
            P(),
            P(),
            P("tower", "mp", None, None),
            P("tower", "mp", None, None),
            P("tower", "mp", None, None),
            P("tower", DP, "mp", None, None),
            P("tower", "mp", DP, None),
        ),
        out_specs=(
            P("tower", "mp", None, None),
            P("tower", "mp", None, None),
            P("tower", DP, "mp", None, None),
            P("tower", "mp", DP, None),
        ),
        check_vma=False,
    )
```

```python
import jax
import jax.numpy as jnp
from jax import lax
from jax.experimental import pallas as pl
from jax.experimental.pallas import tpu as pltpu
from jax.sharding import Mesh, PartitionSpec as P

epsilon = 1e-06
beta_one = 0.9
step_size = 0.01
var_floor = 1e-08

high_shift = 24.0
low_shift = 68.0
low_cap = -30.0
tiny_sum = 8.75e-27


def each_chunk(width, wide, work):
    def step(i, _):
        work(pl.ds(pl.multiple_of(i * wide, wide), wide))
        return 0

    lax.fori_loop(0, width // wide, step, 0)


def core_lanes(core, line):
    return tuple(pl.ds(pl.multiple_of(c * line, 128), line) for c in (core, 1 - core))


def standing(row, count):
    return jnp.broadcast_to(row, (128, count)).T


def lying(column, count):
    return jnp.broadcast_to(column, (count, 128)).T[0:1]


def score_kernel(core_ref, scale_ref, near_ref, far_ref, cols_ref, scores_ref, row_ref, col_ref):
    line = near_ref.shape[0]
    count = scores_ref.shape[0]
    dims = (((1,), (1,)), ((), ()))
    scale = scale_ref[0]
    lanes = core_lanes(core_ref[0], line)
    parts = (slice(0, line), slice(line, count))

    def put(which, value):
        total = jnp.zeros((1, scores_ref.shape[1]), jnp.float32)
        least = jnp.float32(1.0)
        for part, lane in zip(parts, lanes):
            terms = value(part)
            row_sum = lying(jnp.sum(terms, axis=1, keepdims=True), line)
            row_ref[which : which + 1, lane] = row_sum
            least = jnp.minimum(least, jnp.min(row_sum))
            total = total + jnp.sum(terms, axis=0, keepdims=True)
        for copy in range(col_ref.shape[0]):
            col_ref[copy, which : which + 1] = total
        return jnp.minimum(least, jnp.min(total))

    def high_of(part):
        rows_ref = near_ref if part.start == 0 else far_ref
        scores = scale * lax.dot_general(
            rows_ref[...], cols_ref[...], dims, preferred_element_type=jnp.float32
        )
        scores_ref[part] = scores
        return jnp.exp(scores - high_shift)

    least = put(0, high_of)
    row_ref[1:2] = jnp.zeros((1, count), jnp.float32)
    for copy in range(col_ref.shape[0]):
        col_ref[copy, 1:2] = jnp.zeros((1, col_ref.shape[2]), jnp.float32)

    @pl.when(least < tiny_sum)
    def _():
        put(1, lambda part: jnp.exp(jnp.minimum(scores_ref[part], low_cap) + low_shift))


def scored(core, scale, near, far, cols, copies):
    line, width = near.shape
    count = cols.shape[0]
    return pl.pallas_call(
        score_kernel,
        in_specs=[pl.BlockSpec(memory_space=pltpu.SMEM)] * 2
        + [pl.BlockSpec(memory_space=pltpu.VMEM)] * 3,
        out_specs=[pl.BlockSpec(memory_space=pltpu.VMEM)] * 3,
        out_shape=[
            jax.ShapeDtypeStruct((2 * line, count), jnp.float32),
            jax.ShapeDtypeStruct((2, 2 * line), jnp.float32),
            jax.ShapeDtypeStruct((copies, 2, count), jnp.float32),
        ],
        compiler_params=pltpu.CompilerParams(vmem_limit_bytes=40 * 2**20),
        cost_estimate=pl.CostEstimate(
            flops=4 * line * count * width,
            bytes_accessed=2 * width * (2 * line + count) + 8 * line * count,
            transcendentals=2 * line * count,
        ),
    )(core, scale, near, far, cols)


def inverses(sums):
    is_high = sums[0:1] >= tiny_sum
    inverse = 1.0 / jnp.where(is_high, sums[0:1], sums[1:2])
    return jnp.where(is_high, inverse, 0.0), jnp.where(is_high, 0.0, inverse)


def slope_kernel(
    core_ref, scale_ref, scores_ref, row_sum_ref, row_target_ref, col_sum_ref, col_index_ref,
    near_ref, far_ref, col_out, slope_ref
):
    line = near_ref.shape[0]
    count = scores_ref.shape[0]
    near_lanes, far_lanes = core_lanes(core_ref[0], line)
    row_sums = jnp.concatenate([row_sum_ref[:, near_lanes], row_sum_ref[:, far_lanes]], 1)
    row_high, row_low = inverses(row_sums)
    col_high, col_low = inverses(col_sum_ref[...])
    target = standing(row_target_ref[...], count)[:, 0:1] == col_index_ref[...]
    aim = jnp.where(target, 2.0, 0.0)
    factor = 0.5 * scale_ref[0]
    high = jnp.exp(scores_ref[...] - high_shift)
    probs = high * (standing(row_high, count)[:, 0:1] + col_high)
    slope_ref[...] = ((probs - aim) * factor).astype(jnp.bfloat16)

    @pl.when(jnp.maximum(jnp.max(row_low), jnp.max(col_low)) > 0.0)
    def _():
        high = jnp.exp(scores_ref[...] - high_shift)
        probs = high * (standing(row_high, count)[:, 0:1] + col_high)
        low = jnp.exp(jnp.minimum(scores_ref[...], low_cap) + low_shift)
        both = probs + low * (standing(row_low, count)[:, 0:1] + col_low)
        slope_ref[...] = ((both - aim) * factor).astype(jnp.bfloat16)

    dims = (((0,), (0,)), ((), ()))

    def fill(chunk):
        col_out[:, chunk] = (
            lax.dot_general(
                slope_ref[:line], near_ref[:, chunk], dims, preferred_element_type=jnp.float32
            )
            + lax.dot_general(
                slope_ref[line:], far_ref[:, chunk], dims, preferred_element_type=jnp.float32
            )
        ).astype(jnp.bfloat16)

    each_chunk(near_ref.shape[1], 256, fill)


def sloped(core, scale, scores, row_sums, row_target, col_sums, col_index, near, far):
    line, width = near.shape
    count = scores.shape[1]
    return pl.pallas_call(
        slope_kernel,
        in_specs=[pl.BlockSpec(memory_space=pltpu.SMEM)] * 2
        + [pl.BlockSpec(memory_space=pltpu.VMEM)] * 7,
        out_specs=[pl.BlockSpec(memory_space=pltpu.VMEM)] * 2,
        out_shape=[
            jax.ShapeDtypeStruct((count, width), jnp.bfloat16),
            jax.ShapeDtypeStruct(scores.shape, jnp.bfloat16),
        ],
        compiler_params=pltpu.CompilerParams(vmem_limit_bytes=32 * 2**20),
        cost_estimate=pl.CostEstimate(
            flops=4 * line * count * width,
            bytes_accessed=2 * width * (2 * line + count) + 12 * line * count,
            transcendentals=2 * line * count,
        ),
    )(core, scale, scores, row_sums, row_target, col_sums, col_index, near, far)


def row_kernel(slope_ref, cols_ref, near_out, far_out):
    line = near_out.shape[0]
    wide = 256
    for out, rows in ((far_out, slice(line, 2 * line)), (near_out, slice(0, line))):
        for start in range(0, cols_ref.shape[1], wide):
            part = slice(start, start + wide)
            out[:, part] = jnp.dot(
                slope_ref[rows], cols_ref[:, part], preferred_element_type=jnp.float32
            ).astype(jnp.bfloat16)


def row_grads(slope, cols):
    count, width = cols.shape
    out = jax.ShapeDtypeStruct((slope.shape[0] // 2, width), jnp.bfloat16)
    return pl.pallas_call(
        row_kernel,
        in_specs=[pl.BlockSpec(memory_space=pltpu.VMEM)] * 2,
        out_specs=[pl.BlockSpec(memory_space=pltpu.VMEM)] * 2,
        out_shape=[out, out],
        compiler_params=pltpu.CompilerParams(vmem_limit_bytes=24 * 2**20),
        cost_estimate=pl.CostEstimate(
            flops=2 * slope.size * width,
            bytes_accessed=2 * slope.size + 4 * count * width,
            transcendentals=0,
        ),
    )(slope, cols)


def join_kernel(mp_ref, *refs):
    pieces, out_ref = refs[:-1], refs[-1]
    count, rows = len(pieces), pieces[0].shape[0]
    for k, piece in enumerate(pieces):
        start = pl.multiple_of(lax.rem(mp_ref[0] + k, count) * rows, 16)
        out_ref[pl.ds(start, rows)] = piece[...]


def joined(mp, pieces):
    rows, width = pieces[0].shape
    return pl.pallas_call(
        join_kernel,
        in_specs=[pl.BlockSpec(memory_space=pltpu.SMEM)]
        + [pl.BlockSpec(memory_space=pltpu.VMEM)] * len(pieces),
        out_specs=pl.BlockSpec(memory_space=pltpu.VMEM),
        out_shape=jax.ShapeDtypeStruct((rows * len(pieces), width), pieces[0].dtype),
        compiler_params=pltpu.CompilerParams(vmem_limit_bytes=16 * 2**20),
        cost_estimate=pl.CostEstimate(
            flops=0, bytes_accessed=4 * rows * len(pieces) * width, transcendentals=0
        ),
    )(mp, *pieces)


def part_kernel(mp_ref, near_ref, far_ref, *outs):
    count, rows = len(outs), outs[0].shape[0]
    for k, out in enumerate(outs):
        start = pl.multiple_of(lax.rem(mp_ref[0] + k, count) * rows, 16)
        block = pl.ds(start, rows)
        total = near_ref[block].astype(jnp.float32) + far_ref[block].astype(jnp.float32)
        out[...] = total.astype(out.dtype)


def parted(mp, near, far, count):
    rows, width = near.shape[0] // count, near.shape[1]
    return pl.pallas_call(
        part_kernel,
        in_specs=[pl.BlockSpec(memory_space=pltpu.SMEM)]
        + [pl.BlockSpec(memory_space=pltpu.VMEM)] * 2,
        out_specs=[pl.BlockSpec(memory_space=pltpu.VMEM)] * count,
        out_shape=[jax.ShapeDtypeStruct((rows, width), near.dtype)] * count,
        compiler_params=pltpu.CompilerParams(vmem_limit_bytes=16 * 2**20),
        cost_estimate=pl.CostEstimate(
            flops=near.size, bytes_accessed=6 * near.size, transcendentals=0
        ),
    )(mp, near, far)


def owner_rows(mp, tower, k, part, owners, half):
    which = tower if part else 1 - tower
    start = (lax.rem(mp + k, owners) * 2 + which) * half
    return pl.ds(pl.multiple_of(start, 16), half)


def project_kernel(mp_ref, tower_ref, image_ref, text_ref, weight_ref, *refs):
    outs, (raw_ref,) = refs[:-1], refs[-1:]
    half, width = outs[0].shape
    wide = 256
    dims = (((0,), (0,)), ((), ()))

    def fill(feats_ref):
        count = feats_ref.shape[0]
        for start in range(0, width, wide):
            part = slice(start, start + wide)
            raw_ref[:, part] = lax.dot_general(
                feats_ref[...],
                weight_ref[:count, part].astype(jnp.bfloat16),
                dims,
                preferred_element_type=jnp.float32,
            ).astype(jnp.bfloat16)

    @pl.when(tower_ref[0] == 0)
    def _():
        fill(image_ref)

    @pl.when(tower_ref[0] != 0)
    def _():
        fill(text_ref)

    owners = len(outs) // 2
    for n, out in enumerate(outs):
        out[...] = raw_ref[owner_rows(mp_ref[0], tower_ref[0], n // 2, n % 2, owners, half)]


def projected(mp, tower, image, text, weight, owners):
    rows, width = image.shape[1], weight.shape[1]
    half = rows // (2 * owners)
    return pl.pallas_call(
        project_kernel,
        in_specs=[pl.BlockSpec(memory_space=pltpu.SMEM)] * 2
        + [pl.BlockSpec(memory_space=pltpu.VMEM)] * 3,
        out_specs=[pl.BlockSpec(memory_space=pltpu.VMEM)] * (2 * owners),
        out_shape=[jax.ShapeDtypeStruct((half, width), jnp.bfloat16)] * (2 * owners),
        scratch_shapes=[pltpu.VMEM((rows, width), jnp.bfloat16)],
        compiler_params=pltpu.CompilerParams(vmem_limit_bytes=32 * 2**20),
        cost_estimate=pl.CostEstimate(
            flops=2 * rows * weight.size, bytes_accessed=4 * rows * width, transcendentals=0
        ),
    )(mp, tower, image, text, weight)


def grad_kernel(mp_ref, tower_ref, core_ref, image_ref, text_ref, carried_ref, *refs):
    pieces = refs[:-5]
    worker_ref, mine_ref, other_ref, lift_ref, rest_ref = refs[-5:]
    half = pieces[0].shape[0]
    shard_rows, width = worker_ref.shape
    blocks = 2 * mine_ref.shape[0]
    row_block = shard_rows // blocks
    owners = len(pieces) // 2
    for n, piece in enumerate(pieces):
        lift_ref[owner_rows(mp_ref[0], tower_ref[0], n // 2, n % 2, owners, half)] = piece[...]
    wide = 256

    def fill(feats_ref):
        count = feats_ref.shape[0]
        for start in range(0, width, wide):
            part = slice(start, start + wide)
            grad = jnp.dot(
                feats_ref[...], lift_ref[:, part], preferred_element_type=jnp.float32
            )
            worker_ref[:count, part] = (1.0 - beta_one) * grad + carried_ref[:count, part]
        if count < shard_rows:
            worker_ref[count:] = carried_ref[count:]

    @pl.when(tower_ref[0] == 0)
    def _():
        fill(image_ref)

    @pl.when(tower_ref[0] != 0)
    def _():
        fill(text_ref)

    comp = worker_ref[...]
    row_abs = jnp.sum(jnp.abs(comp), axis=1, keepdims=True)
    row = lax.broadcasted_iota(jnp.int32, (shard_rows, 1), 0)
    scale = jnp.zeros((shard_rows, 1), jnp.float32)
    for b in range(blocks):
        inside = (row >= b * row_block) & (row < (b + 1) * row_block)
        total = jnp.sum(jnp.where(inside, row_abs, 0.0), axis=0, keepdims=True)
        scale = jnp.where(inside, total / (row_block * width), scale)
    scale = jnp.broadcast_to(scale, (shard_rows, 128)).astype(jnp.bfloat16).astype(jnp.float32)
    scale = scale[:, 0:1]
    ramp = jnp.clip(comp / (scale + epsilon), -1.0, 1.0).astype(jnp.bfloat16)
    restored = scale * ramp.astype(jnp.float32)
    worker_ref[...] = comp - restored
    tall = mine_ref.shape[1]
    rest_ref[:shard_rows] = restored
    rest_ref[shard_rows:] = jnp.zeros((rest_ref.shape[0] - shard_rows, width), jnp.float32)
    valid = lax.broadcasted_iota(jnp.int32, (tall, 1), 0) < row_block
    even = core_ref[0] == 0
    for b in range(blocks // 2):
        first = 2 * b * row_block
        one = jnp.where(valid, rest_ref[first : first + tall], 0.0)
        two = jnp.where(valid, rest_ref[first + row_block : first + row_block + tall], 0.0)
        mine_ref[b] = jnp.where(even, one, two).astype(jnp.bfloat16)
        other_ref[b] = jnp.where(even, two, one).astype(jnp.bfloat16)


def graded(mp, tower, core, image, text, carried, pieces, blocks):
    shard_rows, width = carried.shape
    rows = image.shape[1]
    sent = jax.ShapeDtypeStruct((blocks // 2, 16, width), jnp.bfloat16)
    return pl.pallas_call(
        grad_kernel,
        in_specs=[pl.BlockSpec(memory_space=pltpu.SMEM)] * 3
        + [pl.BlockSpec(memory_space=pltpu.VMEM)] * (3 + len(pieces)),
        out_specs=[pl.BlockSpec(memory_space=pltpu.VMEM)] * 3,
        out_shape=[jax.ShapeDtypeStruct(carried.shape, jnp.float32), sent, sent],
        scratch_shapes=[
            pltpu.VMEM((rows, width), jnp.bfloat16),
            pltpu.VMEM((shard_rows + 16, width), jnp.float32),
        ],
        compiler_params=pltpu.CompilerParams(vmem_limit_bytes=32 * 2**20),
        cost_estimate=pl.CostEstimate(
            flops=2 * rows * shard_rows * width,
            bytes_accessed=2 * rows * width + 12 * shard_rows * width,
            transcendentals=0,
        ),
    )(mp, tower, core, image, text, carried, *pieces)


def server_kernel(got_ref, error_ref, new_ref, reply_ref, rest_ref):
    row_block, width = error_ref.shape
    halves = got_ref.shape[0]
    total = got_ref[0].astype(jnp.float32)
    for b in range(1, halves):
        total = total + got_ref[b].astype(jnp.float32)
    rest_ref[...] = total
    average = rest_ref[:row_block] / (2 * halves) + error_ref[...]
    scale = jnp.sum(jnp.sum(jnp.abs(average), axis=1, keepdims=True), axis=0, keepdims=True)
    scale = jnp.broadcast_to(scale / (row_block * width), (16, width))
    scale = scale.astype(jnp.bfloat16).astype(jnp.float32)
    ramp = jnp.clip(average / (scale[:row_block] + epsilon), -1.0, 1.0).astype(jnp.bfloat16)
    ramp = ramp.astype(jnp.float32)
    new_ref[...] = average - scale[:row_block] * ramp
    rest_ref[...] = scale
    rest_ref[:row_block] = ramp
    reply = rest_ref[...].astype(jnp.bfloat16)
    for b in range(halves):
        reply_ref[b] = reply


def served(got, error):
    return pl.pallas_call(
        server_kernel,
        in_specs=[pl.BlockSpec(memory_space=pltpu.VMEM)] * 2,
        out_specs=[pl.BlockSpec(memory_space=pltpu.VMEM)] * 2,
        out_shape=[
            jax.ShapeDtypeStruct(error.shape, jnp.float32),
            jax.ShapeDtypeStruct(got.shape, jnp.bfloat16),
        ],
        scratch_shapes=[pltpu.VMEM(got.shape[1:], jnp.float32)],
        compiler_params=pltpu.CompilerParams(vmem_limit_bytes=16 * 2**20),
        cost_estimate=pl.CostEstimate(
            flops=got.size, bytes_accessed=4 * got.size, transcendentals=0
        ),
    )(got, error)


def update_kernel(core_ref, near_ref, far_ref, params_ref, rate_ref, weights_ref, moment_ref):
    halves = near_ref.shape[0]
    row_block = params_ref.shape[0] // (2 * halves)
    even = core_ref[0] == 0
    for b in range(halves):
        near = near_ref[b].astype(jnp.float32)
        far = far_ref[b].astype(jnp.float32)
        for c, block in enumerate((jnp.where(even, near, far), jnp.where(even, far, near))):
            first = (2 * b + c) * row_block
            rows = slice(first, first + row_block)
            moment_ref[rows] = block[:row_block] * block[row_block : row_block + 1]
    weights_ref[...] = params_ref[...] - rate_ref[...] * moment_ref[...]


def updated(core, near, far, params, rate):
    shape = jax.ShapeDtypeStruct(params.shape, jnp.float32)
    return pl.pallas_call(
        update_kernel,
        in_specs=[pl.BlockSpec(memory_space=pltpu.SMEM)]
        + [pl.BlockSpec(memory_space=pltpu.VMEM)] * 4,
        out_specs=[pl.BlockSpec(memory_space=pltpu.VMEM)] * 2,
        out_shape=[shape, shape],
        compiler_params=pltpu.CompilerParams(vmem_limit_bytes=32 * 2**20),
        cost_estimate=pl.CostEstimate(
            flops=3 * params.size, bytes_accessed=20 * params.size, transcendentals=0
        ),
    )(core, near, far, params, rate)


XY = ("tower", "xh", "y")
X2 = ("xh", "y")
DP = ("xh", "y", "core")


def shifted(block, axis, count, shift):
    return lax.ppermute(block, axis, [((i + shift) % count, i) for i in range(count)])


def crossed(block, axis, count, flip):
    return lax.ppermute(block, axis, [(i, i ^ flip) for i in range(count)])


def from_each(blocks, axis):
    return lax.all_to_all(blocks, axis, split_axis=0, concat_axis=0, tiled=True)


def ring_blocks(block, axis, count, direct=None):
    blocks = [block] * count
    if direct:
        blocks[direct] = shifted(block, axis, count, direct)
    ahead = behind = block
    for step in range(1, count // 2 + 1):
        if count - step != direct:
            behind = blocks[count - step] = shifted(behind, axis, count, -1)
        if step < count // 2:
            ahead = blocks[step] = shifted(ahead, axis, count, 1)
    return blocks


def ring_sum(term, axis, count, direct=None):
    wide, narrow = jnp.float32, jnp.bfloat16
    far = count // 2 - 1 if direct else count // 2
    ahead = term(far)
    for k in range(far - 1, -1, -1):
        ahead = shifted(ahead.astype(narrow), axis, count, -1).astype(wide) + term(k)
    behind = term(count // 2 + 1)
    for k in range(count // 2 + 2, count):
        behind = shifted(behind.astype(narrow), axis, count, 1).astype(wide) + term(k)
    total = ahead + shifted(behind.astype(narrow), axis, count, 1).astype(wide)
    if direct:
        total = total + shifted(term(direct).astype(narrow), axis, count, -direct).astype(wide)
    return total


def body(
    image_feats,
    text_feats,
    labels,
    logit_scale,
    params,
    momentum,
    variance,
    worker_error,
    server_error,
):
    tower = lax.axis_index("tower")
    x_hi = lax.axis_index("xh")
    y = lax.axis_index("y")
    core = lax.axis_index("core")
    mp = lax.axis_index("mp")
    mp_count = lax.axis_size("mp")
    dp_count = lax.axis_size(DP)
    xy_count = lax.axis_size(XY)
    group_rows = image_feats.shape[0]
    per_dev = group_rows // mp_count
    half = per_dev // 2
    line = mp_count * half
    text_width = text_feats.shape[1]
    shard_rows = params.shape[2]
    width = params.shape[3]
    row_block = shard_rows // dp_count
    is_image = tower == 0
    f32, bf16 = jnp.float32, jnp.bfloat16

    mp_at, tower_at, core_at = (i.astype(jnp.int32).reshape(1) for i in (mp, tower, core))
    image, text = image_feats.T, text_feats.T
    partial = projected(mp_at, tower_at, image, text, params[0, 0], mp_count)

    def embedded(part):
        raw = ring_sum(lambda k: partial[2 * k + part].astype(f32), "mp", mp_count)
        norm = jnp.sqrt(jnp.sum(raw * raw, axis=1, keepdims=True) + epsilon)
        unit = raw / norm
        return unit, norm, unit.astype(bf16)

    out_unit, out_norm, out_emb = embedded(0)
    swapped = crossed(out_emb, "tower", 2, 1)
    kept_unit, kept_norm, kept = embedded(1)
    image_own = jnp.where(is_image, kept, swapped)
    text_own = jnp.where(is_image, swapped, kept)

    cols = from_each(
        jnp.broadcast_to(text_own[None], (xy_count, half, width)), XY
    ).reshape(xy_count * half, width)
    near = joined(mp_at, ring_blocks(image_own, "mp", mp_count, mp_count // 2))
    far = crossed(near, "core", 2, 1)

    place = (x_hi * 4 + y) * 2
    label_blocks = labels.reshape(dp_count, mp_count, 2, half)

    def line_labels(which_core):
        one = lax.dynamic_index_in_dim(label_blocks, place + which_core, 0, False)
        return lax.dynamic_index_in_dim(one, tower, 1, False).reshape(1, -1)

    row_target = jnp.concatenate([line_labels(core), line_labels(1 - core)], 1).astype(f32)
    owner = jnp.arange(xy_count, dtype=jnp.int32)
    col_index = (
        ((owner % 8 * 2 + core) * group_rows + mp * per_dev + owner // 8 * half)[:, None]
        + jnp.arange(half, dtype=jnp.int32)[None, :]
    ).reshape(1, -1).astype(f32)
    row_target, col_index = lax.optimization_barrier((row_target, col_index))

    carried = beta_one * momentum[0, 0] + worker_error[0, 0, 0]
    rate = step_size / (jnp.sqrt(variance[0, 0]) + var_floor)
    cols, carried, rate = lax.optimization_barrier((cols, carried, rate))

    scores, row_sums, col_sums = scored(core_at, logit_scale, near, far, cols, xy_count)

    col_sums = jnp.sum(from_each(col_sums, XY), axis=0)
    row_sums = lax.psum(row_sums + crossed(row_sums, "core", 2, 1), "mp")

    col_part, slope = sloped(
        core_at, logit_scale, scores, row_sums, row_target, col_sums, col_index, near, far
    )
    near_part, far_part = row_grads(slope, cols)

    passed = crossed(far_part, "core", 2, 1)
    text_grad = jnp.sum(
        from_each(col_part.reshape(xy_count, half, width), XY).astype(f32), axis=0
    )
    sent = parted(mp_at, near_part, passed, mp_count)
    image_grad = ring_sum(lambda k: sent[k].astype(f32), "mp", mp_count)

    kept_grad = jnp.where(is_image, image_grad, text_grad)
    out_grad = crossed(
        jnp.where(is_image, text_grad, image_grad).astype(bf16), "tower", 2, 1
    ).astype(f32)

    def lifted(unit, norm, grad):
        inner = jnp.sum(unit * grad, axis=1, keepdims=True)
        return ((grad - unit * inner) / norm).astype(bf16)

    kept_blocks = ring_blocks(lifted(kept_unit, kept_norm, kept_grad), "mp", mp_count)
    out_blocks = ring_blocks(lifted(out_unit, out_norm, out_grad), "mp", mp_count)
    worker_new, mine, other = graded(
        mp_at,
        tower_at,
        core_at,
        image,
        text,
        carried,
        [block for both in zip(out_blocks, kept_blocks) for block in both],
        dp_count,
    )

    pair = mine.astype(f32) + crossed(other, "core", 2, 1).astype(f32)
    server_new, reply = served(from_each(pair.astype(bf16), X2), server_error[0, 0])
    near_reply = from_each(reply, X2)
    far_reply = crossed(near_reply, "core", 2, 1)
    weights_new, momentum_new = updated(core_at, near_reply, far_reply, params[0, 0], rate)
    return (
        weights_new[None, None],
        momentum_new[None, None],
        worker_new[None, None, None],
        server_new[None, None],
    )


def solution(mesh):
    fine = Mesh(mesh.devices.reshape(2, 2, 4, 2, 8), ("tower", "xh", "y", "core", "mp"))
    return jax.shard_map(
        body,
        mesh=fine,
        in_specs=(
            P(DP, "mp"),
            P(DP, "mp"),
            P(),
            P(),
            P("tower", "mp", None, None),
            P("tower", "mp", None, None),
            P("tower", "mp", None, None),
            P("tower", DP, "mp", None, None),
            P("tower", "mp", DP, None),
        ),
        out_specs=(
            P("tower", "mp", None, None),
            P("tower", "mp", None, None),
            P("tower", DP, "mp", None, None),
            P("tower", "mp", DP, None),
        ),
        check_vma=False,
    )
```

```python
import jax
import jax.numpy as jnp
from jax import lax
from jax.experimental import pallas as pl
from jax.experimental.pallas import tpu as pltpu
from jax.sharding import Mesh, PartitionSpec as P

epsilon = 1e-06
beta_one = 0.9
step_size = 0.01
var_floor = 1e-08

high_shift = 24.0
low_shift = 68.0
low_cap = -30.0
tiny_sum = 8.75e-27


def core_lanes(core, line):
    return tuple(pl.ds(pl.multiple_of(c * line, 128), line) for c in (core, 1 - core))


def standing(row, count):
    return jnp.broadcast_to(row, (128, count)).T


def lying(column, count):
    return jnp.broadcast_to(column, (count, 128)).T[0:1]


def score_kernel(core_ref, scale_ref, near_ref, far_ref, cols_ref, row_ref, col_ref, scores_ref):
    line = near_ref.shape[0]
    count = scores_ref.shape[0]
    dims = (((1,), (1,)), ((), ()))
    scale = scale_ref[0]
    lanes = core_lanes(core_ref[0], line)
    parts = (slice(0, line), slice(line, count))

    def put(which, value):
        total = jnp.zeros((1, scores_ref.shape[1]), jnp.float32)
        least = jnp.float32(1.0)
        for part, lane in zip(parts, lanes):
            terms = value(part)
            row_sum = lying(jnp.sum(terms, axis=1, keepdims=True), line)
            row_ref[which : which + 1, lane] = row_sum
            least = jnp.minimum(least, jnp.min(row_sum))
            total = total + jnp.sum(terms, axis=0, keepdims=True)
        for copy in range(col_ref.shape[0]):
            col_ref[copy, which : which + 1] = total
        return jnp.minimum(least, jnp.min(total))

    def high_of(part):
        rows_ref = near_ref if part.start == 0 else far_ref
        scores = scale * lax.dot_general(
            rows_ref[...], cols_ref[...], dims, preferred_element_type=jnp.float32
        )
        scores_ref[part] = scores
        return jnp.exp(scores - high_shift)

    least = put(0, high_of)
    row_ref[1:2] = jnp.zeros((1, count), jnp.float32)
    for copy in range(col_ref.shape[0]):
        col_ref[copy, 1:2] = jnp.zeros((1, col_ref.shape[2]), jnp.float32)

    @pl.when(least < tiny_sum)
    def _():
        put(1, lambda part: jnp.exp(jnp.minimum(scores_ref[part], low_cap) + low_shift))


def scored(core, scale, near, far, cols, copies):
    line, width = near.shape
    count = cols.shape[0]
    return pl.pallas_call(
        score_kernel,
        in_specs=[pl.BlockSpec(memory_space=pltpu.SMEM)] * 2
        + [pl.BlockSpec(memory_space=pltpu.VMEM)] * 3,
        out_specs=[pl.BlockSpec(memory_space=pltpu.VMEM)] * 2,
        out_shape=[
            jax.ShapeDtypeStruct((2, 2 * line), jnp.float32),
            jax.ShapeDtypeStruct((copies, 2, count), jnp.float32),
        ],
        scratch_shapes=[pltpu.VMEM((2 * line, count), jnp.float32)],
        compiler_params=pltpu.CompilerParams(vmem_limit_bytes=40 * 2**20),
        cost_estimate=pl.CostEstimate(
            flops=4 * line * count * width,
            bytes_accessed=2 * width * (2 * line + count) + 8 * line * count,
            transcendentals=2 * line * count,
        ),
    )(core, scale, near, far, cols)


def inverses(sums):
    is_high = sums[0:1] >= tiny_sum
    inverse = 1.0 / jnp.where(is_high, sums[0:1], sums[1:2])
    return jnp.where(is_high, inverse, 0.0), jnp.where(is_high, 0.0, inverse)


def slope_kernel(
    core_ref, scale_ref, row_sum_ref, row_target_ref, col_sum_ref, col_index_ref,
    near_ref, far_ref, cols_ref, near_out, far_out, col_out, slope_ref, scores_ref
):
    line = near_ref.shape[0]
    count = cols_ref.shape[0]
    scale = scale_ref[0]
    col_sums = col_sum_ref[0]
    for copy in range(1, col_sum_ref.shape[0]):
        col_sums = col_sums + col_sum_ref[copy]
    col_high, col_low = inverses(col_sums)
    dims = (((1,), (1,)), ((), ()))
    wide = 256
    halves = (
        (far_ref, far_out, slice(line, 2 * line), 1),
        (near_ref, near_out, slice(0, line), 0),
    )
    lanes = core_lanes(core_ref[0], line)
    for rows_ref, out, part, which in halves:
        scores = scale * lax.dot_general(
            rows_ref[...], cols_ref[...], dims, preferred_element_type=jnp.float32
        )
        scores_ref[...] = scores
        row_high, row_low = inverses(row_sum_ref[:, lanes[which]])
        target = standing(row_target_ref[:, part], line)[:, 0:1] == col_index_ref[...]
        aim = jnp.where(target, 2.0, 0.0)
        factor = 0.5 * scale
        probs = jnp.exp(scores - high_shift) * (standing(row_high, line)[:, 0:1] + col_high)
        slope_ref[part] = ((probs - aim) * factor).astype(jnp.bfloat16)

        @pl.when(jnp.maximum(jnp.max(row_low), jnp.max(col_low)) > 0.0)
        def _():
            scores = scores_ref[...]
            high = jnp.exp(scores - high_shift) * (standing(row_high, line)[:, 0:1] + col_high)
            low = jnp.exp(jnp.minimum(scores, low_cap) + low_shift)
            both = high + low * (standing(row_low, line)[:, 0:1] + col_low)
            slope_ref[part] = ((both - aim) * factor).astype(jnp.bfloat16)

        for start in range(0, cols_ref.shape[1], wide):
            block = slice(start, start + wide)
            out[:, block] = jnp.dot(
                slope_ref[part], cols_ref[:, block], preferred_element_type=jnp.float32
            ).astype(jnp.bfloat16)

    dims = (((0,), (0,)), ((), ()))
    for start in range(0, cols_ref.shape[1], wide):
        block = slice(start, start + wide)
        col_out[:, block] = (
            lax.dot_general(
                slope_ref[:line], near_ref[:, block], dims, preferred_element_type=jnp.float32
            )
            + lax.dot_general(
                slope_ref[line:], far_ref[:, block], dims, preferred_element_type=jnp.float32
            )
        ).astype(jnp.bfloat16)


def sloped(core, scale, row_sums, row_target, col_sums, col_index, near, far, cols):
    line, width = near.shape
    count = cols.shape[0]
    out = jax.ShapeDtypeStruct((line, width), jnp.bfloat16)
    return pl.pallas_call(
        slope_kernel,
        in_specs=[pl.BlockSpec(memory_space=pltpu.SMEM)] * 2
        + [pl.BlockSpec(memory_space=pltpu.VMEM)] * 7,
        out_specs=[pl.BlockSpec(memory_space=pltpu.VMEM)] * 3,
        out_shape=[out, out, jax.ShapeDtypeStruct(cols.shape, jnp.bfloat16)],
        scratch_shapes=[
            pltpu.VMEM((2 * line, count), jnp.bfloat16),
            pltpu.VMEM((line, count), jnp.float32),
        ],
        compiler_params=pltpu.CompilerParams(vmem_limit_bytes=32 * 2**20),
        cost_estimate=pl.CostEstimate(
            flops=12 * line * count * width,
            bytes_accessed=4 * width * (2 * line + count),
            transcendentals=2 * line * count,
        ),
    )(core, scale, row_sums, row_target, col_sums, col_index, near, far, cols)


def join_kernel(mp_ref, *refs):
    pieces, out_ref = refs[:-1], refs[-1]
    count, rows = len(pieces), pieces[0].shape[0]
    for k, piece in enumerate(pieces):
        start = pl.multiple_of(lax.rem(mp_ref[0] + k, count) * rows, 16)
        out_ref[pl.ds(start, rows)] = piece[...]


def joined(mp, pieces):
    rows, width = pieces[0].shape
    return pl.pallas_call(
        join_kernel,
        in_specs=[pl.BlockSpec(memory_space=pltpu.SMEM)]
        + [pl.BlockSpec(memory_space=pltpu.VMEM)] * len(pieces),
        out_specs=pl.BlockSpec(memory_space=pltpu.VMEM),
        out_shape=jax.ShapeDtypeStruct((rows * len(pieces), width), pieces[0].dtype),
        compiler_params=pltpu.CompilerParams(vmem_limit_bytes=16 * 2**20),
        cost_estimate=pl.CostEstimate(
            flops=0, bytes_accessed=4 * rows * len(pieces) * width, transcendentals=0
        ),
    )(mp, *pieces)


def part_kernel(mp_ref, near_ref, far_ref, *outs):
    count, rows = len(outs), outs[0].shape[0]
    for k, out in enumerate(outs):
        start = pl.multiple_of(lax.rem(mp_ref[0] + k, count) * rows, 16)
        block = pl.ds(start, rows)
        total = near_ref[block].astype(jnp.float32) + far_ref[block].astype(jnp.float32)
        out[...] = total.astype(out.dtype)


def parted(mp, near, far, count):
    rows, width = near.shape[0] // count, near.shape[1]
    return pl.pallas_call(
        part_kernel,
        in_specs=[pl.BlockSpec(memory_space=pltpu.SMEM)]
        + [pl.BlockSpec(memory_space=pltpu.VMEM)] * 2,
        out_specs=[pl.BlockSpec(memory_space=pltpu.VMEM)] * count,
        out_shape=[jax.ShapeDtypeStruct((rows, width), near.dtype)] * count,
        compiler_params=pltpu.CompilerParams(vmem_limit_bytes=16 * 2**20),
        cost_estimate=pl.CostEstimate(
            flops=near.size, bytes_accessed=6 * near.size, transcendentals=0
        ),
    )(mp, near, far)


def owner_rows(mp, tower, k, part, owners, half):
    which = tower if part else 1 - tower
    start = (lax.rem(mp + k, owners) * 2 + which) * half
    return pl.ds(pl.multiple_of(start, 16), half)


def project_kernel(mp_ref, tower_ref, image_ref, text_ref, weight_ref, *refs):
    outs, (raw_ref,) = refs[:-1], refs[-1:]
    half, width = outs[0].shape
    wide = 256
    dims = (((0,), (0,)), ((), ()))

    def fill(feats_ref):
        count = feats_ref.shape[0]
        for start in range(0, width, wide):
            part = slice(start, start + wide)
            raw_ref[:, part] = lax.dot_general(
                feats_ref[...],
                weight_ref[:count, part].astype(jnp.bfloat16),
                dims,
                preferred_element_type=jnp.float32,
            ).astype(jnp.bfloat16)

    @pl.when(tower_ref[0] == 0)
    def _():
        fill(image_ref)

    @pl.when(tower_ref[0] != 0)
    def _():
        fill(text_ref)

    owners = len(outs) // 2
    for n, out in enumerate(outs):
        out[...] = raw_ref[owner_rows(mp_ref[0], tower_ref[0], n // 2, n % 2, owners, half)]


def projected(mp, tower, image, text, weight, owners):
    rows, width = image.shape[1], weight.shape[1]
    half = rows // (2 * owners)
    return pl.pallas_call(
        project_kernel,
        in_specs=[pl.BlockSpec(memory_space=pltpu.SMEM)] * 2
        + [pl.BlockSpec(memory_space=pltpu.VMEM)] * 3,
        out_specs=[pl.BlockSpec(memory_space=pltpu.VMEM)] * (2 * owners),
        out_shape=[jax.ShapeDtypeStruct((half, width), jnp.bfloat16)] * (2 * owners),
        scratch_shapes=[pltpu.VMEM((rows, width), jnp.bfloat16)],
        compiler_params=pltpu.CompilerParams(vmem_limit_bytes=32 * 2**20),
        cost_estimate=pl.CostEstimate(
            flops=2 * rows * weight.size, bytes_accessed=4 * rows * width, transcendentals=0
        ),
    )(mp, tower, image, text, weight)


def grad_kernel(mp_ref, tower_ref, core_ref, image_ref, text_ref, carried_ref, *refs):
    pieces = refs[:-5]
    worker_ref, mine_ref, other_ref, lift_ref, rest_ref = refs[-5:]
    half = pieces[0].shape[0]
    shard_rows, width = worker_ref.shape
    blocks = 2 * mine_ref.shape[0]
    row_block = shard_rows // blocks
    owners = len(pieces) // 2
    for n, piece in enumerate(pieces):
        lift_ref[owner_rows(mp_ref[0], tower_ref[0], n // 2, n % 2, owners, half)] = piece[...]
    wide = 256

    def fill(feats_ref):
        count = feats_ref.shape[0]
        for start in range(0, width, wide):
            part = slice(start, start + wide)
            grad = jnp.dot(
                feats_ref[...], lift_ref[:, part], preferred_element_type=jnp.float32
            )
            worker_ref[:count, part] = (1.0 - beta_one) * grad + carried_ref[:count, part]
        if count < shard_rows:
            worker_ref[count:] = carried_ref[count:]

    @pl.when(tower_ref[0] == 0)
    def _():
        fill(image_ref)

    @pl.when(tower_ref[0] != 0)
    def _():
        fill(text_ref)

    comp = worker_ref[...]
    row_abs = jnp.sum(jnp.abs(comp), axis=1, keepdims=True)
    row = lax.broadcasted_iota(jnp.int32, (shard_rows, 1), 0)
    scale = jnp.zeros((shard_rows, 1), jnp.float32)
    for b in range(blocks):
        inside = (row >= b * row_block) & (row < (b + 1) * row_block)
        total = jnp.sum(jnp.where(inside, row_abs, 0.0), axis=0, keepdims=True)
        scale = jnp.where(inside, total / (row_block * width), scale)
    scale = jnp.broadcast_to(scale, (shard_rows, 128)).astype(jnp.bfloat16).astype(jnp.float32)
    scale = scale[:, 0:1]
    ramp = jnp.clip(comp / (scale + epsilon), -1.0, 1.0).astype(jnp.bfloat16)
    restored = scale * ramp.astype(jnp.float32)
    worker_ref[...] = comp - restored
    tall = mine_ref.shape[1]
    rest_ref[:shard_rows] = restored
    rest_ref[shard_rows:] = jnp.zeros((rest_ref.shape[0] - shard_rows, width), jnp.float32)
    valid = lax.broadcasted_iota(jnp.int32, (tall, 1), 0) < row_block
    even = core_ref[0] == 0
    for b in range(blocks // 2):
        first = 2 * b * row_block
        one = jnp.where(valid, rest_ref[first : first + tall], 0.0)
        two = jnp.where(valid, rest_ref[first + row_block : first + row_block + tall], 0.0)
        mine_ref[b] = jnp.where(even, one, two).astype(jnp.bfloat16)
        other_ref[b] = jnp.where(even, two, one).astype(jnp.bfloat16)


def graded(mp, tower, core, image, text, carried, pieces, blocks):
    shard_rows, width = carried.shape
    rows = image.shape[1]
    sent = jax.ShapeDtypeStruct((blocks // 2, 16, width), jnp.bfloat16)
    return pl.pallas_call(
        grad_kernel,
        in_specs=[pl.BlockSpec(memory_space=pltpu.SMEM)] * 3
        + [pl.BlockSpec(memory_space=pltpu.VMEM)] * (3 + len(pieces)),
        out_specs=[pl.BlockSpec(memory_space=pltpu.VMEM)] * 3,
        out_shape=[jax.ShapeDtypeStruct(carried.shape, jnp.float32), sent, sent],
        scratch_shapes=[
            pltpu.VMEM((rows, width), jnp.bfloat16),
            pltpu.VMEM((shard_rows + 16, width), jnp.float32),
        ],
        compiler_params=pltpu.CompilerParams(vmem_limit_bytes=32 * 2**20),
        cost_estimate=pl.CostEstimate(
            flops=2 * rows * shard_rows * width,
            bytes_accessed=2 * rows * width + 12 * shard_rows * width,
            transcendentals=0,
        ),
    )(mp, tower, core, image, text, carried, *pieces)


def server_kernel(got_ref, error_ref, new_ref, reply_ref, rest_ref):
    row_block, width = error_ref.shape
    halves = got_ref.shape[0]
    total = got_ref[0].astype(jnp.float32)
    for b in range(1, halves):
        total = total + got_ref[b].astype(jnp.float32)
    rest_ref[...] = total
    average = rest_ref[:row_block] / (2 * halves) + error_ref[...]
    scale = jnp.sum(jnp.sum(jnp.abs(average), axis=1, keepdims=True), axis=0, keepdims=True)
    scale = jnp.broadcast_to(scale / (row_block * width), (16, width))
    scale = scale.astype(jnp.bfloat16).astype(jnp.float32)
    ramp = jnp.clip(average / (scale[:row_block] + epsilon), -1.0, 1.0).astype(jnp.bfloat16)
    ramp = ramp.astype(jnp.float32)
    new_ref[...] = average - scale[:row_block] * ramp
    rest_ref[...] = scale
    rest_ref[:row_block] = ramp
    reply = rest_ref[...].astype(jnp.bfloat16)
    for b in range(halves):
        reply_ref[b] = reply


def served(got, error):
    return pl.pallas_call(
        server_kernel,
        in_specs=[pl.BlockSpec(memory_space=pltpu.VMEM)] * 2,
        out_specs=[pl.BlockSpec(memory_space=pltpu.VMEM)] * 2,
        out_shape=[
            jax.ShapeDtypeStruct(error.shape, jnp.float32),
            jax.ShapeDtypeStruct(got.shape, jnp.bfloat16),
        ],
        scratch_shapes=[pltpu.VMEM(got.shape[1:], jnp.float32)],
        compiler_params=pltpu.CompilerParams(vmem_limit_bytes=16 * 2**20),
        cost_estimate=pl.CostEstimate(
            flops=got.size, bytes_accessed=4 * got.size, transcendentals=0
        ),
    )(got, error)


def update_kernel(core_ref, near_ref, far_ref, params_ref, rate_ref, weights_ref, moment_ref):
    halves = near_ref.shape[0]
    row_block = params_ref.shape[0] // (2 * halves)
    even = core_ref[0] == 0
    for b in range(halves):
        near = near_ref[b].astype(jnp.float32)
        far = far_ref[b].astype(jnp.float32)
        for c, block in enumerate((jnp.where(even, near, far), jnp.where(even, far, near))):
            first = (2 * b + c) * row_block
            rows = slice(first, first + row_block)
            moment_ref[rows] = block[:row_block] * block[row_block : row_block + 1]
    weights_ref[...] = params_ref[...] - rate_ref[...] * moment_ref[...]


def updated(core, near, far, params, rate):
    shape = jax.ShapeDtypeStruct(params.shape, jnp.float32)
    return pl.pallas_call(
        update_kernel,
        in_specs=[pl.BlockSpec(memory_space=pltpu.SMEM)]
        + [pl.BlockSpec(memory_space=pltpu.VMEM)] * 4,
        out_specs=[pl.BlockSpec(memory_space=pltpu.VMEM)] * 2,
        out_shape=[shape, shape],
        compiler_params=pltpu.CompilerParams(vmem_limit_bytes=32 * 2**20),
        cost_estimate=pl.CostEstimate(
            flops=3 * params.size, bytes_accessed=20 * params.size, transcendentals=0
        ),
    )(core, near, far, params, rate)


XY = ("tower", "xh", "y")
X2 = ("xh", "y")
DP = ("xh", "y", "core")


def shifted(block, axis, count, shift):
    return lax.ppermute(block, axis, [((i + shift) % count, i) for i in range(count)])


def crossed(block, axis, count, flip):
    return lax.ppermute(block, axis, [(i, i ^ flip) for i in range(count)])


def from_each(blocks, axis):
    return lax.all_to_all(blocks, axis, split_axis=0, concat_axis=0, tiled=True)


def ring_blocks(block, axis, count, direct=None):
    blocks = [block] * count
    if direct:
        blocks[direct] = shifted(block, axis, count, direct)
    ahead = behind = block
    for step in range(1, count // 2 + 1):
        if count - step != direct:
            behind = blocks[count - step] = shifted(behind, axis, count, -1)
        if step < count // 2:
            ahead = blocks[step] = shifted(ahead, axis, count, 1)
    return blocks


def ring_sum(term, axis, count, direct=None):
    wide, narrow = jnp.float32, jnp.bfloat16
    far = count // 2 - 1 if direct else count // 2
    ahead = term(far)
    for k in range(far - 1, -1, -1):
        ahead = shifted(ahead.astype(narrow), axis, count, -1).astype(wide) + term(k)
    behind = term(count // 2 + 1)
    for k in range(count // 2 + 2, count):
        behind = shifted(behind.astype(narrow), axis, count, 1).astype(wide) + term(k)
    total = ahead + shifted(behind.astype(narrow), axis, count, 1).astype(wide)
    if direct:
        total = total + shifted(term(direct).astype(narrow), axis, count, -direct).astype(wide)
    return total


def body(
    image_feats,
    text_feats,
    labels,
    logit_scale,
    params,
    momentum,
    variance,
    worker_error,
    server_error,
):
    tower = lax.axis_index("tower")
    x_hi = lax.axis_index("xh")
    y = lax.axis_index("y")
    core = lax.axis_index("core")
    mp = lax.axis_index("mp")
    mp_count = lax.axis_size("mp")
    dp_count = lax.axis_size(DP)
    xy_count = lax.axis_size(XY)
    group_rows = image_feats.shape[0]
    per_dev = group_rows // mp_count
    half = per_dev // 2
    line = mp_count * half
    text_width = text_feats.shape[1]
    shard_rows = params.shape[2]
    width = params.shape[3]
    row_block = shard_rows // dp_count
    is_image = tower == 0
    f32, bf16 = jnp.float32, jnp.bfloat16

    mp_at, tower_at, core_at = (i.astype(jnp.int32).reshape(1) for i in (mp, tower, core))
    image, text = image_feats.T, text_feats.T
    partial = projected(mp_at, tower_at, image, text, params[0, 0], mp_count)

    def embedded(part):
        raw = ring_sum(lambda k: partial[2 * k + part].astype(f32), "mp", mp_count)
        norm = jnp.sqrt(jnp.sum(raw * raw, axis=1, keepdims=True) + epsilon)
        unit = raw / norm
        return unit, norm, unit.astype(bf16)

    out_unit, out_norm, out_emb = embedded(0)
    swapped = crossed(out_emb, "tower", 2, 1)
    kept_unit, kept_norm, kept = embedded(1)
    image_own = jnp.where(is_image, kept, swapped)
    text_own = jnp.where(is_image, swapped, kept)

    cols = from_each(
        jnp.broadcast_to(text_own[None], (xy_count, half, width)), XY
    ).reshape(xy_count * half, width)
    near = joined(mp_at, ring_blocks(image_own, "mp", mp_count, mp_count // 2))
    far = crossed(near, "core", 2, 1)

    place = (x_hi * 4 + y) * 2
    label_blocks = labels.reshape(dp_count, mp_count, 2, half)

    def line_labels(which_core):
        one = lax.dynamic_index_in_dim(label_blocks, place + which_core, 0, False)
        return lax.dynamic_index_in_dim(one, tower, 1, False).reshape(1, -1)

    row_target = jnp.concatenate([line_labels(core), line_labels(1 - core)], 1).astype(f32)
    owner = jnp.arange(xy_count, dtype=jnp.int32)
    col_index = (
        ((owner % 8 * 2 + core) * group_rows + mp * per_dev + owner // 8 * half)[:, None]
        + jnp.arange(half, dtype=jnp.int32)[None, :]
    ).reshape(1, -1).astype(f32)
    row_target, col_index = lax.optimization_barrier((row_target, col_index))

    carried = beta_one * momentum[0, 0] + worker_error[0, 0, 0]
    rate = step_size / (jnp.sqrt(variance[0, 0]) + var_floor)
    cols, carried, rate = lax.optimization_barrier((cols, carried, rate))

    row_sums, col_sums = scored(core_at, logit_scale, near, far, cols, xy_count)

    col_sums = from_each(col_sums, XY)
    row_sums = lax.psum(row_sums + crossed(row_sums, "core", 2, 1), "mp")

    near_part, far_part, col_part = sloped(
        core_at, logit_scale, row_sums, row_target, col_sums, col_index, near, far, cols
    )

    passed = crossed(far_part, "core", 2, 1)
    text_grad = jnp.sum(
        from_each(col_part.reshape(xy_count, half, width), XY).astype(f32), axis=0
    )
    sent = parted(mp_at, near_part, passed, mp_count)
    image_grad = ring_sum(lambda k: sent[k].astype(f32), "mp", mp_count)

    kept_grad = jnp.where(is_image, image_grad, text_grad)
    out_grad = crossed(
        jnp.where(is_image, text_grad, image_grad).astype(bf16), "tower", 2, 1
    ).astype(f32)

    def lifted(unit, norm, grad):
        inner = jnp.sum(unit * grad, axis=1, keepdims=True)
        return ((grad - unit * inner) / norm).astype(bf16)

    kept_blocks = ring_blocks(lifted(kept_unit, kept_norm, kept_grad), "mp", mp_count)
    out_blocks = ring_blocks(lifted(out_unit, out_norm, out_grad), "mp", mp_count)
    worker_new, mine, other = graded(
        mp_at,
        tower_at,
        core_at,
        image,
        text,
        carried,
        [block for both in zip(out_blocks, kept_blocks) for block in both],
        dp_count,
    )

    pair = mine.astype(f32) + crossed(other, "core", 2, 1).astype(f32)
    server_new, reply = served(from_each(pair.astype(bf16), X2), server_error[0, 0])
    near_reply = from_each(reply, X2)
    far_reply = crossed(near_reply, "core", 2, 1)
    weights_new, momentum_new = updated(core_at, near_reply, far_reply, params[0, 0], rate)
    return (
        weights_new[None, None],
        momentum_new[None, None],
        worker_new[None, None, None],
        server_new[None, None],
    )


def solution(mesh):
    fine = Mesh(mesh.devices.reshape(2, 2, 4, 2, 8), ("tower", "xh", "y", "core", "mp"))
    return jax.shard_map(
        body,
        mesh=fine,
        in_specs=(
            P(DP, "mp"),
            P(DP, "mp"),
            P(),
            P(),
            P("tower", "mp", None, None),
            P("tower", "mp", None, None),
            P("tower", "mp", None, None),
            P("tower", DP, "mp", None, None),
            P("tower", "mp", DP, None),
        ),
        out_specs=(
            P("tower", "mp", None, None),
            P("tower", "mp", None, None),
            P("tower", DP, "mp", None, None),
            P("tower", "mp", DP, None),
        ),
        check_vma=False,
    )
```

```python
import jax
import jax.numpy as jnp
from jax import lax
from jax.experimental import pallas as pl
from jax.experimental.pallas import tpu as pltpu
from jax.sharding import Mesh, PartitionSpec as P

epsilon = 1e-06
beta_one = 0.9
step_size = 0.01
var_floor = 1e-08

high_shift = 24.0
low_shift = 68.0
low_cap = -30.0
tiny_sum = 8.75e-27


def core_lanes(core, line):
    return tuple(pl.ds(pl.multiple_of(c * line, 128), line) for c in (core, 1 - core))


def standing(row, count):
    return jnp.broadcast_to(row, (128, count)).T


def lying(column, count):
    return jnp.broadcast_to(column, (count, 128)).T[0:1]


def score_kernel(core_ref, scale_ref, near_ref, far_ref, cols_ref, row_ref, col_ref, scores_ref):
    line = near_ref.shape[0]
    count = scores_ref.shape[0]
    dims = (((1,), (1,)), ((), ()))
    scale = scale_ref[0]
    lanes = core_lanes(core_ref[0], line)
    parts = (slice(0, line), slice(line, count))

    def put(which, value):
        total = jnp.zeros((1, scores_ref.shape[1]), jnp.float32)
        least = jnp.float32(1.0)
        for part, lane in zip(parts, lanes):
            terms = value(part)
            row_sum = lying(jnp.sum(terms, axis=1, keepdims=True), line)
            row_ref[which : which + 1, lane] = row_sum
            least = jnp.minimum(least, jnp.min(row_sum))
            total = total + jnp.sum(terms, axis=0, keepdims=True)
        for copy in range(col_ref.shape[0]):
            col_ref[copy, which : which + 1] = total
        return jnp.minimum(least, jnp.min(total))

    def high_of(part):
        rows_ref = near_ref if part.start == 0 else far_ref
        scores = scale * lax.dot_general(
            rows_ref[...], cols_ref[...], dims, preferred_element_type=jnp.float32
        )
        scores_ref[part] = scores
        return jnp.exp(scores - high_shift)

    least = put(0, high_of)
    row_ref[1:2] = jnp.zeros((1, count), jnp.float32)
    for copy in range(col_ref.shape[0]):
        col_ref[copy, 1:2] = jnp.zeros((1, col_ref.shape[2]), jnp.float32)

    @pl.when(least < tiny_sum)
    def _():
        put(1, lambda part: jnp.exp(jnp.minimum(scores_ref[part], low_cap) + low_shift))


def scored(core, scale, near, far, cols, copies):
    line, width = near.shape
    count = cols.shape[0]
    return pl.pallas_call(
        score_kernel,
        in_specs=[pl.BlockSpec(memory_space=pltpu.SMEM)] * 2
        + [pl.BlockSpec(memory_space=pltpu.VMEM)] * 3,
        out_specs=[pl.BlockSpec(memory_space=pltpu.VMEM)] * 2,
        out_shape=[
            jax.ShapeDtypeStruct((2, 2 * line), jnp.float32),
            jax.ShapeDtypeStruct((copies, 2, count), jnp.float32),
        ],
        scratch_shapes=[pltpu.VMEM((2 * line, count), jnp.float32)],
        compiler_params=pltpu.CompilerParams(vmem_limit_bytes=40 * 2**20),
        cost_estimate=pl.CostEstimate(
            flops=4 * line * count * width,
            bytes_accessed=2 * width * (2 * line + count) + 8 * line * count,
            transcendentals=2 * line * count,
        ),
    )(core, scale, near, far, cols)


def inverses(sums):
    is_high = sums[0:1] >= tiny_sum
    inverse = 1.0 / jnp.where(is_high, sums[0:1], sums[1:2])
    return jnp.where(is_high, inverse, 0.0), jnp.where(is_high, 0.0, inverse)


def slope_kernel(
    core_ref, scale_ref, row_sum_ref, row_target_ref, col_sum_ref, col_index_ref,
    near_ref, far_ref, cols_ref, near_out, far_out, col_out, slope_ref, scores_ref
):
    line = near_ref.shape[0]
    count = cols_ref.shape[0]
    scale = scale_ref[0]
    col_sums = col_sum_ref[0]
    for copy in range(1, col_sum_ref.shape[0]):
        col_sums = col_sums + col_sum_ref[copy]
    col_high, col_low = inverses(col_sums)
    dims = (((1,), (1,)), ((), ()))
    wide = 256
    halves = (
        (far_ref, far_out, slice(line, 2 * line), 1),
        (near_ref, near_out, slice(0, line), 0),
    )
    lanes = core_lanes(core_ref[0], line)
    for rows_ref, out, part, which in halves:
        scores = scale * lax.dot_general(
            rows_ref[...], cols_ref[...], dims, preferred_element_type=jnp.float32
        )
        scores_ref[...] = scores
        row_high, row_low = inverses(row_sum_ref[:, lanes[which]])
        target = standing(row_target_ref[:, part], line)[:, 0:1] == col_index_ref[...]
        aim = jnp.where(target, 2.0, 0.0)
        factor = 0.5 * scale
        probs = jnp.exp(scores - high_shift) * (standing(row_high, line)[:, 0:1] + col_high)
        slope_ref[part] = ((probs - aim) * factor).astype(jnp.bfloat16)

        @pl.when(jnp.maximum(jnp.max(row_low), jnp.max(col_low)) > 0.0)
        def _():
            scores = scores_ref[...]
            high = jnp.exp(scores - high_shift) * (standing(row_high, line)[:, 0:1] + col_high)
            low = jnp.exp(jnp.minimum(scores, low_cap) + low_shift)
            both = high + low * (standing(row_low, line)[:, 0:1] + col_low)
            slope_ref[part] = ((both - aim) * factor).astype(jnp.bfloat16)

        for start in range(0, cols_ref.shape[1], wide):
            block = slice(start, start + wide)
            out[:, block] = jnp.dot(
                slope_ref[part], cols_ref[:, block], preferred_element_type=jnp.float32
            ).astype(jnp.bfloat16)

    dims = (((0,), (0,)), ((), ()))
    for start in range(0, cols_ref.shape[1], wide):
        block = slice(start, start + wide)
        col_out[:, block] = (
            lax.dot_general(
                slope_ref[:line], near_ref[:, block], dims, preferred_element_type=jnp.float32
            )
            + lax.dot_general(
                slope_ref[line:], far_ref[:, block], dims, preferred_element_type=jnp.float32
            )
        ).astype(jnp.bfloat16)


def sloped(core, scale, row_sums, row_target, col_sums, col_index, near, far, cols):
    line, width = near.shape
    count = cols.shape[0]
    out = jax.ShapeDtypeStruct((line, width), jnp.bfloat16)
    return pl.pallas_call(
        slope_kernel,
        in_specs=[pl.BlockSpec(memory_space=pltpu.SMEM)] * 2
        + [pl.BlockSpec(memory_space=pltpu.VMEM)] * 7,
        out_specs=[pl.BlockSpec(memory_space=pltpu.VMEM)] * 3,
        out_shape=[out, out, jax.ShapeDtypeStruct(cols.shape, jnp.bfloat16)],
        scratch_shapes=[
            pltpu.VMEM((2 * line, count), jnp.bfloat16),
            pltpu.VMEM((line, count), jnp.float32),
        ],
        compiler_params=pltpu.CompilerParams(vmem_limit_bytes=32 * 2**20),
        cost_estimate=pl.CostEstimate(
            flops=12 * line * count * width,
            bytes_accessed=4 * width * (2 * line + count),
            transcendentals=2 * line * count,
        ),
    )(core, scale, row_sums, row_target, col_sums, col_index, near, far, cols)


def join_kernel(mp_ref, *refs):
    pieces, out_ref = refs[:-1], refs[-1]
    count, rows = len(pieces), pieces[0].shape[0]
    for k, piece in enumerate(pieces):
        start = pl.multiple_of(lax.rem(mp_ref[0] + k, count) * rows, 16)
        out_ref[pl.ds(start, rows)] = piece[...]


def joined(mp, pieces):
    rows, width = pieces[0].shape
    return pl.pallas_call(
        join_kernel,
        in_specs=[pl.BlockSpec(memory_space=pltpu.SMEM)]
        + [pl.BlockSpec(memory_space=pltpu.VMEM)] * len(pieces),
        out_specs=pl.BlockSpec(memory_space=pltpu.VMEM),
        out_shape=jax.ShapeDtypeStruct((rows * len(pieces), width), pieces[0].dtype),
        compiler_params=pltpu.CompilerParams(vmem_limit_bytes=16 * 2**20),
        cost_estimate=pl.CostEstimate(
            flops=0, bytes_accessed=4 * rows * len(pieces) * width, transcendentals=0
        ),
    )(mp, *pieces)


def part_kernel(mp_ref, near_ref, far_ref, *outs):
    count, rows = len(outs), outs[0].shape[0]
    for k, out in enumerate(outs):
        start = pl.multiple_of(lax.rem(mp_ref[0] + k, count) * rows, 16)
        block = pl.ds(start, rows)
        total = near_ref[block].astype(jnp.float32) + far_ref[block].astype(jnp.float32)
        out[...] = total.astype(out.dtype)


def parted(mp, near, far, count):
    rows, width = near.shape[0] // count, near.shape[1]
    return pl.pallas_call(
        part_kernel,
        in_specs=[pl.BlockSpec(memory_space=pltpu.SMEM)]
        + [pl.BlockSpec(memory_space=pltpu.VMEM)] * 2,
        out_specs=[pl.BlockSpec(memory_space=pltpu.VMEM)] * count,
        out_shape=[jax.ShapeDtypeStruct((rows, width), near.dtype)] * count,
        compiler_params=pltpu.CompilerParams(vmem_limit_bytes=16 * 2**20),
        cost_estimate=pl.CostEstimate(
            flops=near.size, bytes_accessed=6 * near.size, transcendentals=0
        ),
    )(mp, near, far)


def owner_rows(mp, tower, k, part, owners, half):
    which = tower if part else 1 - tower
    start = (lax.rem(mp + k, owners) * 2 + which) * half
    return pl.ds(pl.multiple_of(start, 16), half)


def project_kernel(mp_ref, tower_ref, image_ref, text_ref, weight_ref, *refs):
    outs, (raw_ref,) = refs[:-1], refs[-1:]
    half, width = outs[0].shape
    wide = 256
    dims = (((0,), (0,)), ((), ()))

    def fill(feats_ref):
        count = feats_ref.shape[0]
        for start in range(0, width, wide):
            part = slice(start, start + wide)
            raw_ref[:, part] = lax.dot_general(
                feats_ref[...],
                weight_ref[:count, part].astype(jnp.bfloat16),
                dims,
                preferred_element_type=jnp.float32,
            ).astype(jnp.bfloat16)

    @pl.when(tower_ref[0] == 0)
    def _():
        fill(image_ref)

    @pl.when(tower_ref[0] != 0)
    def _():
        fill(text_ref)

    owners = len(outs) // 2
    for n, out in enumerate(outs):
        out[...] = raw_ref[owner_rows(mp_ref[0], tower_ref[0], n // 2, n % 2, owners, half)]


def projected(mp, tower, image, text, weight, owners):
    rows, width = image.shape[1], weight.shape[1]
    half = rows // (2 * owners)
    return pl.pallas_call(
        project_kernel,
        in_specs=[pl.BlockSpec(memory_space=pltpu.SMEM)] * 2
        + [pl.BlockSpec(memory_space=pltpu.VMEM)] * 3,
        out_specs=[pl.BlockSpec(memory_space=pltpu.VMEM)] * (2 * owners),
        out_shape=[jax.ShapeDtypeStruct((half, width), jnp.bfloat16)] * (2 * owners),
        scratch_shapes=[pltpu.VMEM((rows, width), jnp.bfloat16)],
        compiler_params=pltpu.CompilerParams(vmem_limit_bytes=32 * 2**20),
        cost_estimate=pl.CostEstimate(
            flops=2 * rows * weight.size, bytes_accessed=4 * rows * width, transcendentals=0
        ),
    )(mp, tower, image, text, weight)


def grad_kernel(mp_ref, tower_ref, core_ref, image_ref, text_ref, carried_ref, *refs):
    pieces = refs[:-5]
    worker_ref, mine_ref, other_ref, lift_ref, rest_ref = refs[-5:]
    half = pieces[0].shape[0]
    shard_rows, width = worker_ref.shape
    blocks = 2 * mine_ref.shape[0]
    row_block = shard_rows // blocks
    owners = len(pieces) // 2
    for n, piece in enumerate(pieces):
        lift_ref[owner_rows(mp_ref[0], tower_ref[0], n // 2, n % 2, owners, half)] = piece[...]
    wide = 256

    def fill(feats_ref):
        count = feats_ref.shape[0]
        for start in range(0, width, wide):
            part = slice(start, start + wide)
            grad = jnp.dot(
                feats_ref[...], lift_ref[:, part], preferred_element_type=jnp.float32
            )
            worker_ref[:count, part] = (1.0 - beta_one) * grad + carried_ref[:count, part]
        if count < shard_rows:
            worker_ref[count:] = carried_ref[count:]

    @pl.when(tower_ref[0] == 0)
    def _():
        fill(image_ref)

    @pl.when(tower_ref[0] != 0)
    def _():
        fill(text_ref)

    comp = worker_ref[...]
    row_abs = jnp.sum(jnp.abs(comp), axis=1, keepdims=True)
    row = lax.broadcasted_iota(jnp.int32, (shard_rows, 1), 0)
    scale = jnp.zeros((shard_rows, 1), jnp.float32)
    for b in range(blocks):
        inside = (row >= b * row_block) & (row < (b + 1) * row_block)
        total = jnp.sum(jnp.where(inside, row_abs, 0.0), axis=0, keepdims=True)
        scale = jnp.where(inside, total / (row_block * width), scale)
    scale = jnp.broadcast_to(scale, (shard_rows, 128)).astype(jnp.bfloat16).astype(jnp.float32)
    scale = scale[:, 0:1]
    ramp = jnp.clip(comp / (scale + epsilon), -1.0, 1.0).astype(jnp.bfloat16)
    restored = scale * ramp.astype(jnp.float32)
    worker_ref[...] = comp - restored
    tall = mine_ref.shape[1]
    rest_ref[:shard_rows] = restored
    rest_ref[shard_rows:] = jnp.zeros((rest_ref.shape[0] - shard_rows, width), jnp.float32)
    valid = lax.broadcasted_iota(jnp.int32, (tall, 1), 0) < row_block
    even = core_ref[0] == 0
    for b in range(blocks // 2):
        first = 2 * b * row_block
        one = jnp.where(valid, rest_ref[first : first + tall], 0.0)
        two = jnp.where(valid, rest_ref[first + row_block : first + row_block + tall], 0.0)
        mine_ref[b] = jnp.where(even, one, two).astype(jnp.bfloat16)
        other_ref[b] = jnp.where(even, two, one).astype(jnp.bfloat16)


def graded(mp, tower, core, image, text, carried, pieces, blocks):
    shard_rows, width = carried.shape
    rows = image.shape[1]
    sent = jax.ShapeDtypeStruct((blocks // 2, 16, width), jnp.bfloat16)
    return pl.pallas_call(
        grad_kernel,
        in_specs=[pl.BlockSpec(memory_space=pltpu.SMEM)] * 3
        + [pl.BlockSpec(memory_space=pltpu.VMEM)] * (3 + len(pieces)),
        out_specs=[pl.BlockSpec(memory_space=pltpu.VMEM)] * 3,
        out_shape=[jax.ShapeDtypeStruct(carried.shape, jnp.float32), sent, sent],
        scratch_shapes=[
            pltpu.VMEM((rows, width), jnp.bfloat16),
            pltpu.VMEM((shard_rows + 16, width), jnp.float32),
        ],
        compiler_params=pltpu.CompilerParams(vmem_limit_bytes=32 * 2**20),
        cost_estimate=pl.CostEstimate(
            flops=2 * rows * shard_rows * width,
            bytes_accessed=2 * rows * width + 12 * shard_rows * width,
            transcendentals=0,
        ),
    )(mp, tower, core, image, text, carried, *pieces)


def server_kernel(got_ref, error_ref, new_ref, reply_ref, rest_ref):
    row_block, width = error_ref.shape
    halves = got_ref.shape[0]
    total = got_ref[0].astype(jnp.float32)
    for b in range(1, halves):
        total = total + got_ref[b].astype(jnp.float32)
    rest_ref[...] = total
    average = rest_ref[:row_block] / (2 * halves) + error_ref[...]
    scale = jnp.sum(jnp.sum(jnp.abs(average), axis=1, keepdims=True), axis=0, keepdims=True)
    scale = jnp.broadcast_to(scale / (row_block * width), (16, width))
    scale = scale.astype(jnp.bfloat16).astype(jnp.float32)
    ramp = jnp.clip(average / (scale[:row_block] + epsilon), -1.0, 1.0).astype(jnp.bfloat16)
    ramp = ramp.astype(jnp.float32)
    new_ref[...] = average - scale[:row_block] * ramp
    rest_ref[...] = scale
    rest_ref[:row_block] = ramp
    reply = rest_ref[...].astype(jnp.bfloat16)
    for b in range(halves):
        reply_ref[b] = reply


def served(got, error):
    return pl.pallas_call(
        server_kernel,
        in_specs=[pl.BlockSpec(memory_space=pltpu.VMEM)] * 2,
        out_specs=[pl.BlockSpec(memory_space=pltpu.VMEM)] * 2,
        out_shape=[
            jax.ShapeDtypeStruct(error.shape, jnp.float32),
            jax.ShapeDtypeStruct(got.shape, jnp.bfloat16),
        ],
        scratch_shapes=[pltpu.VMEM(got.shape[1:], jnp.float32)],
        compiler_params=pltpu.CompilerParams(vmem_limit_bytes=16 * 2**20),
        cost_estimate=pl.CostEstimate(
            flops=got.size, bytes_accessed=4 * got.size, transcendentals=0
        ),
    )(got, error)


def update_kernel(core_ref, near_ref, far_ref, params_ref, rate_ref, weights_ref, moment_ref):
    halves = near_ref.shape[0]
    row_block = params_ref.shape[0] // (2 * halves)
    even = core_ref[0] == 0
    for b in range(halves):
        near = near_ref[b].astype(jnp.float32)
        far = far_ref[b].astype(jnp.float32)
        for c, block in enumerate((jnp.where(even, near, far), jnp.where(even, far, near))):
            first = (2 * b + c) * row_block
            rows = slice(first, first + row_block)
            moment_ref[rows] = block[:row_block] * block[row_block : row_block + 1]
    weights_ref[...] = params_ref[...] - rate_ref[...] * moment_ref[...]


def updated(core, near, far, params, rate):
    shape = jax.ShapeDtypeStruct(params.shape, jnp.float32)
    return pl.pallas_call(
        update_kernel,
        in_specs=[pl.BlockSpec(memory_space=pltpu.SMEM)]
        + [pl.BlockSpec(memory_space=pltpu.VMEM)] * 4,
        out_specs=[pl.BlockSpec(memory_space=pltpu.VMEM)] * 2,
        out_shape=[shape, shape],
        compiler_params=pltpu.CompilerParams(vmem_limit_bytes=32 * 2**20),
        cost_estimate=pl.CostEstimate(
            flops=3 * params.size, bytes_accessed=20 * params.size, transcendentals=0
        ),
    )(core, near, far, params, rate)


XY = ("tower", "xh", "y")
X2 = ("xh", "y")
DP = ("xh", "y", "core")


def shifted(block, axis, count, shift):
    return lax.ppermute(block, axis, [((i + shift) % count, i) for i in range(count)])


def crossed(block, axis, count, flip):
    return lax.ppermute(block, axis, [(i, i ^ flip) for i in range(count)])


def from_each(blocks, axis):
    return lax.all_to_all(blocks, axis, split_axis=0, concat_axis=0, tiled=True)


def ring_blocks(block, axis, count, ahead_count, direct=()):
    blocks = [block] * count
    for k in direct:
        blocks[k] = shifted(block, axis, count, k)
    ahead = behind = block
    for k in range(1, count):
        if k <= ahead_count and k not in direct:
            ahead = blocks[k] = shifted(ahead, axis, count, 1)
        if count - k > ahead_count and count - k not in direct:
            behind = blocks[count - k] = shifted(behind, axis, count, -1)
    return blocks


def ring_sum(term, axis, count, ahead_count, direct=()):
    wide, narrow = jnp.float32, jnp.bfloat16
    ahead_steps = [k for k in range(1, ahead_count + 1) if k not in direct]
    behind_steps = [k for k in range(ahead_count + 1, count) if k not in direct]
    total = term(0)
    for k in direct:
        total = total + shifted(term(k).astype(narrow), axis, count, -k).astype(wide)
    for steps, shift in ((ahead_steps[::-1], -1), (behind_steps, 1)):
        passed = None
        for k in steps:
            held = term(k) if passed is None else passed + term(k)
            passed = shifted(held.astype(narrow), axis, count, shift).astype(wide)
        total = total + passed
    return total


def body(
    image_feats,
    text_feats,
    labels,
    logit_scale,
    params,
    momentum,
    variance,
    worker_error,
    server_error,
):
    tower = lax.axis_index("tower")
    x_hi = lax.axis_index("xh")
    y = lax.axis_index("y")
    core = lax.axis_index("core")
    mp = lax.axis_index("mp")
    mp_count = lax.axis_size("mp")
    dp_count = lax.axis_size(DP)
    xy_count = lax.axis_size(XY)
    group_rows = image_feats.shape[0]
    per_dev = group_rows // mp_count
    half = per_dev // 2
    line = mp_count * half
    text_width = text_feats.shape[1]
    shard_rows = params.shape[2]
    width = params.shape[3]
    row_block = shard_rows // dp_count
    is_image = tower == 0
    f32, bf16 = jnp.float32, jnp.bfloat16

    mp_at, tower_at, core_at = (i.astype(jnp.int32).reshape(1) for i in (mp, tower, core))
    image, text = image_feats.T, text_feats.T
    partial = projected(mp_at, tower_at, image, text, params[0, 0], mp_count)

    def embedded(part):
        raw = ring_sum(lambda k: partial[2 * k + part].astype(f32), "mp", mp_count, 4)
        norm = jnp.sqrt(jnp.sum(raw * raw, axis=1, keepdims=True) + epsilon)
        unit = raw / norm
        return unit, norm, unit.astype(bf16)

    out_unit, out_norm, out_emb = embedded(0)
    swapped = crossed(out_emb, "tower", 2, 1)
    kept_unit, kept_norm, kept = embedded(1)
    image_own = jnp.where(is_image, kept, swapped)
    text_own = jnp.where(is_image, swapped, kept)

    cols = from_each(
        jnp.broadcast_to(text_own[None], (xy_count, half, width)), XY
    ).reshape(xy_count * half, width)
    near = joined(mp_at, ring_blocks(image_own, "mp", mp_count, 4, (4,)))
    far = crossed(near, "core", 2, 1)

    place = (x_hi * 4 + y) * 2
    label_blocks = labels.reshape(dp_count, mp_count, 2, half)

    def line_labels(which_core):
        one = lax.dynamic_index_in_dim(label_blocks, place + which_core, 0, False)
        return lax.dynamic_index_in_dim(one, tower, 1, False).reshape(1, -1)

    row_target = jnp.concatenate([line_labels(core), line_labels(1 - core)], 1).astype(f32)
    owner = jnp.arange(xy_count, dtype=jnp.int32)
    col_index = (
        ((owner % 8 * 2 + core) * group_rows + mp * per_dev + owner // 8 * half)[:, None]
        + jnp.arange(half, dtype=jnp.int32)[None, :]
    ).reshape(1, -1).astype(f32)
    row_target, col_index = lax.optimization_barrier((row_target, col_index))

    carried = beta_one * momentum[0, 0] + worker_error[0, 0, 0]
    rate = step_size / (jnp.sqrt(variance[0, 0]) + var_floor)
    cols, carried, rate = lax.optimization_barrier((cols, carried, rate))

    row_sums, col_sums = scored(core_at, logit_scale, near, far, cols, xy_count)

    col_sums = from_each(col_sums, XY)
    row_sums = lax.psum(row_sums + crossed(row_sums, "core", 2, 1), "mp")

    near_part, far_part, col_part = sloped(
        core_at, logit_scale, row_sums, row_target, col_sums, col_index, near, far, cols
    )

    passed = crossed(far_part, "core", 2, 1)
    text_grad = jnp.sum(
        from_each(col_part.reshape(xy_count, half, width), XY).astype(f32), axis=0
    )
    sent = parted(mp_at, near_part, passed, mp_count)
    image_grad = ring_sum(lambda k: sent[k].astype(f32), "mp", mp_count, 4, (4, 3, 5))

    kept_grad = jnp.where(is_image, image_grad, text_grad)
    out_grad = crossed(
        jnp.where(is_image, text_grad, image_grad).astype(bf16), "tower", 2, 1
    ).astype(f32)

    def lifted(unit, norm, grad):
        inner = jnp.sum(unit * grad, axis=1, keepdims=True)
        return ((grad - unit * inner) / norm).astype(bf16)

    kept_blocks = ring_blocks(lifted(kept_unit, kept_norm, kept_grad), "mp", mp_count, 3)
    out_blocks = ring_blocks(lifted(out_unit, out_norm, out_grad), "mp", mp_count, 4)
    worker_new, mine, other = graded(
        mp_at,
        tower_at,
        core_at,
        image,
        text,
        carried,
        [block for both in zip(out_blocks, kept_blocks) for block in both],
        dp_count,
    )

    pair = mine.astype(f32) + crossed(other, "core", 2, 1).astype(f32)
    server_new, reply = served(from_each(pair.astype(bf16), X2), server_error[0, 0])
    near_reply = from_each(reply, X2)
    far_reply = crossed(near_reply, "core", 2, 1)
    weights_new, momentum_new = updated(core_at, near_reply, far_reply, params[0, 0], rate)
    return (
        weights_new[None, None],
        momentum_new[None, None],
        worker_new[None, None, None],
        server_new[None, None],
    )


def solution(mesh):
    fine = Mesh(mesh.devices.reshape(2, 2, 4, 2, 8), ("tower", "xh", "y", "core", "mp"))
    return jax.shard_map(
        body,
        mesh=fine,
        in_specs=(
            P(DP, "mp"),
            P(DP, "mp"),
            P(),
            P(),
            P("tower", "mp", None, None),
            P("tower", "mp", None, None),
            P("tower", "mp", None, None),
            P("tower", DP, "mp", None, None),
            P("tower", "mp", DP, None),
        ),
        out_specs=(
            P("tower", "mp", None, None),
            P("tower", "mp", None, None),
            P("tower", DP, "mp", None, None),
            P("tower", "mp", DP, None),
        ),
        check_vma=False,
    )
```

```python
import jax
import jax.numpy as jnp
from jax import lax
from jax.experimental import pallas as pl
from jax.experimental.pallas import tpu as pltpu
from jax.sharding import Mesh, PartitionSpec as P

epsilon = 1e-06
beta_one = 0.9
step_size = 0.01
var_floor = 1e-08

high_shift = 24.0
low_shift = 68.0
low_cap = -30.0
tiny_sum = 8.75e-27


def core_lanes(core, line):
    return tuple(pl.ds(pl.multiple_of(c * line, 128), line) for c in (core, 1 - core))


def standing(row, count):
    return jnp.broadcast_to(row, (128, count)).T


def lying(column, count):
    return jnp.broadcast_to(column, (count, 128)).T[0:1]


def score_kernel(core_ref, scale_ref, near_ref, far_ref, cols_ref, row_ref, col_ref, scores_ref):
    line = near_ref.shape[0]
    count = scores_ref.shape[0]
    dims = (((1,), (1,)), ((), ()))
    scale = scale_ref[0]
    lanes = core_lanes(core_ref[0], line)
    parts = (slice(0, line), slice(line, count))

    def put(which, value):
        total = jnp.zeros((1, scores_ref.shape[1]), jnp.float32)
        least = jnp.float32(1.0)
        for part, lane in zip(parts, lanes):
            terms = value(part)
            row_sum = lying(jnp.sum(terms, axis=1, keepdims=True), line)
            row_ref[which : which + 1, lane] = row_sum
            least = jnp.minimum(least, jnp.min(row_sum))
            total = total + jnp.sum(terms, axis=0, keepdims=True)
        for copy in range(col_ref.shape[0]):
            col_ref[copy, which : which + 1] = total
        return jnp.minimum(least, jnp.min(total))

    def high_of(part):
        rows_ref = near_ref if part.start == 0 else far_ref
        scores = scale * lax.dot_general(
            rows_ref[...], cols_ref[...], dims, preferred_element_type=jnp.float32
        )
        scores_ref[part] = scores
        return jnp.exp(scores - high_shift)

    least = put(0, high_of)
    row_ref[1:2] = jnp.zeros((1, count), jnp.float32)
    for copy in range(col_ref.shape[0]):
        col_ref[copy, 1:2] = jnp.zeros((1, col_ref.shape[2]), jnp.float32)

    @pl.when(least < tiny_sum)
    def _():
        put(1, lambda part: jnp.exp(jnp.minimum(scores_ref[part], low_cap) + low_shift))


def scored(core, scale, near, far, cols, copies):
    line, width = near.shape
    count = cols.shape[0]
    return pl.pallas_call(
        score_kernel,
        in_specs=[pl.BlockSpec(memory_space=pltpu.SMEM)] * 2
        + [pl.BlockSpec(memory_space=pltpu.VMEM)] * 3,
        out_specs=[pl.BlockSpec(memory_space=pltpu.VMEM)] * 2,
        out_shape=[
            jax.ShapeDtypeStruct((2, 2 * line), jnp.float32),
            jax.ShapeDtypeStruct((copies, 2, count), jnp.float32),
        ],
        scratch_shapes=[pltpu.VMEM((2 * line, count), jnp.float32)],
        compiler_params=pltpu.CompilerParams(vmem_limit_bytes=40 * 2**20),
        cost_estimate=pl.CostEstimate(
            flops=4 * line * count * width,
            bytes_accessed=2 * width * (2 * line + count) + 8 * line * count,
            transcendentals=2 * line * count,
        ),
    )(core, scale, near, far, cols)


def inverses(sums):
    is_high = sums[0:1] >= tiny_sum
    inverse = 1.0 / jnp.where(is_high, sums[0:1], sums[1:2])
    return jnp.where(is_high, inverse, 0.0), jnp.where(is_high, 0.0, inverse)


def slope_kernel(
    core_ref, scale_ref, row_sum_ref, row_target_ref, col_sum_ref, col_index_ref,
    near_ref, far_ref, cols_ref, near_out, far_out, col_out, slope_ref, scores_ref
):
    line = near_ref.shape[0]
    count = cols_ref.shape[0]
    scale = scale_ref[0]
    col_sums = col_sum_ref[0]
    for copy in range(1, col_sum_ref.shape[0]):
        col_sums = col_sums + col_sum_ref[copy]
    col_high, col_low = inverses(col_sums)
    dims = (((1,), (1,)), ((), ()))
    wide = 256
    halves = (
        (far_ref, far_out, slice(line, 2 * line), 1),
        (near_ref, near_out, slice(0, line), 0),
    )
    lanes = core_lanes(core_ref[0], line)
    for rows_ref, out, part, which in halves:
        scores = scale * lax.dot_general(
            rows_ref[...], cols_ref[...], dims, preferred_element_type=jnp.float32
        )
        scores_ref[...] = scores
        row_high, row_low = inverses(row_sum_ref[:, lanes[which]])
        target = standing(row_target_ref[:, part], line)[:, 0:1] == col_index_ref[...]
        aim = jnp.where(target, 2.0, 0.0)
        factor = 0.5 * scale
        probs = jnp.exp(scores - high_shift) * (standing(row_high, line)[:, 0:1] + col_high)
        slope_ref[part] = ((probs - aim) * factor).astype(jnp.bfloat16)

        @pl.when(jnp.maximum(jnp.max(row_low), jnp.max(col_low)) > 0.0)
        def _():
            scores = scores_ref[...]
            high = jnp.exp(scores - high_shift) * (standing(row_high, line)[:, 0:1] + col_high)
            low = jnp.exp(jnp.minimum(scores, low_cap) + low_shift)
            both = high + low * (standing(row_low, line)[:, 0:1] + col_low)
            slope_ref[part] = ((both - aim) * factor).astype(jnp.bfloat16)

        for start in range(0, cols_ref.shape[1], wide):
            block = slice(start, start + wide)
            out[:, block] = jnp.dot(
                slope_ref[part], cols_ref[:, block], preferred_element_type=jnp.float32
            ).astype(jnp.bfloat16)

    dims = (((0,), (0,)), ((), ()))
    for start in range(0, cols_ref.shape[1], wide):
        block = slice(start, start + wide)
        col_out[:, block] = (
            lax.dot_general(
                slope_ref[:line], near_ref[:, block], dims, preferred_element_type=jnp.float32
            )
            + lax.dot_general(
                slope_ref[line:], far_ref[:, block], dims, preferred_element_type=jnp.float32
            )
        ).astype(jnp.bfloat16)


def sloped(core, scale, row_sums, row_target, col_sums, col_index, near, far, cols):
    line, width = near.shape
    count = cols.shape[0]
    out = jax.ShapeDtypeStruct((line, width), jnp.bfloat16)
    return pl.pallas_call(
        slope_kernel,
        in_specs=[pl.BlockSpec(memory_space=pltpu.SMEM)] * 2
        + [pl.BlockSpec(memory_space=pltpu.VMEM)] * 7,
        out_specs=[pl.BlockSpec(memory_space=pltpu.VMEM)] * 3,
        out_shape=[out, out, jax.ShapeDtypeStruct(cols.shape, jnp.bfloat16)],
        scratch_shapes=[
            pltpu.VMEM((2 * line, count), jnp.bfloat16),
            pltpu.VMEM((line, count), jnp.float32),
        ],
        compiler_params=pltpu.CompilerParams(vmem_limit_bytes=32 * 2**20),
        cost_estimate=pl.CostEstimate(
            flops=12 * line * count * width,
            bytes_accessed=4 * width * (2 * line + count),
            transcendentals=2 * line * count,
        ),
    )(core, scale, row_sums, row_target, col_sums, col_index, near, far, cols)


def join_kernel(mp_ref, *refs):
    pieces, out_ref = refs[:-1], refs[-1]
    count, rows = len(pieces), pieces[0].shape[0]
    for k, piece in enumerate(pieces):
        start = pl.multiple_of(lax.rem(mp_ref[0] + k, count) * rows, 16)
        out_ref[pl.ds(start, rows)] = piece[...]


def joined(mp, pieces):
    rows, width = pieces[0].shape
    return pl.pallas_call(
        join_kernel,
        in_specs=[pl.BlockSpec(memory_space=pltpu.SMEM)]
        + [pl.BlockSpec(memory_space=pltpu.VMEM)] * len(pieces),
        out_specs=pl.BlockSpec(memory_space=pltpu.VMEM),
        out_shape=jax.ShapeDtypeStruct((rows * len(pieces), width), pieces[0].dtype),
        compiler_params=pltpu.CompilerParams(vmem_limit_bytes=16 * 2**20),
        cost_estimate=pl.CostEstimate(
            flops=0, bytes_accessed=4 * rows * len(pieces) * width, transcendentals=0
        ),
    )(mp, *pieces)


def part_kernel(mp_ref, near_ref, far_ref, *outs):
    count, rows = len(outs), outs[0].shape[0]
    for k, out in enumerate(outs):
        start = pl.multiple_of(lax.rem(mp_ref[0] + k, count) * rows, 16)
        block = pl.ds(start, rows)
        total = near_ref[block].astype(jnp.float32) + far_ref[block].astype(jnp.float32)
        out[...] = total.astype(out.dtype)


def parted(mp, near, far, count):
    rows, width = near.shape[0] // count, near.shape[1]
    return pl.pallas_call(
        part_kernel,
        in_specs=[pl.BlockSpec(memory_space=pltpu.SMEM)]
        + [pl.BlockSpec(memory_space=pltpu.VMEM)] * 2,
        out_specs=[pl.BlockSpec(memory_space=pltpu.VMEM)] * count,
        out_shape=[jax.ShapeDtypeStruct((rows, width), near.dtype)] * count,
        compiler_params=pltpu.CompilerParams(vmem_limit_bytes=16 * 2**20),
        cost_estimate=pl.CostEstimate(
            flops=near.size, bytes_accessed=6 * near.size, transcendentals=0
        ),
    )(mp, near, far)


def owner_rows(mp, tower, k, part, owners, half):
    which = tower if part else 1 - tower
    start = (lax.rem(mp + k, owners) * 2 + which) * half
    return pl.ds(pl.multiple_of(start, 16), half)


def project_kernel(mp_ref, tower_ref, image_ref, text_ref, weight_ref, *refs):
    outs, (raw_ref,) = refs[:-1], refs[-1:]
    half, width = outs[0].shape
    wide = 256
    dims = (((0,), (0,)), ((), ()))

    def fill(feats_ref):
        count = feats_ref.shape[0]
        for start in range(0, width, wide):
            part = slice(start, start + wide)
            raw_ref[:, part] = lax.dot_general(
                feats_ref[...],
                weight_ref[:count, part].astype(jnp.bfloat16),
                dims,
                preferred_element_type=jnp.float32,
            ).astype(jnp.bfloat16)

    @pl.when(tower_ref[0] == 0)
    def _():
        fill(image_ref)

    @pl.when(tower_ref[0] != 0)
    def _():
        fill(text_ref)

    owners = len(outs) // 2
    for n, out in enumerate(outs):
        out[...] = raw_ref[owner_rows(mp_ref[0], tower_ref[0], n // 2, n % 2, owners, half)]


def projected(mp, tower, image, text, weight, owners):
    rows, width = image.shape[1], weight.shape[1]
    half = rows // (2 * owners)
    return pl.pallas_call(
        project_kernel,
        in_specs=[pl.BlockSpec(memory_space=pltpu.SMEM)] * 2
        + [pl.BlockSpec(memory_space=pltpu.VMEM)] * 3,
        out_specs=[pl.BlockSpec(memory_space=pltpu.VMEM)] * (2 * owners),
        out_shape=[jax.ShapeDtypeStruct((half, width), jnp.bfloat16)] * (2 * owners),
        scratch_shapes=[pltpu.VMEM((rows, width), jnp.bfloat16)],
        compiler_params=pltpu.CompilerParams(vmem_limit_bytes=32 * 2**20),
        cost_estimate=pl.CostEstimate(
            flops=2 * rows * weight.size, bytes_accessed=4 * rows * width, transcendentals=0
        ),
    )(mp, tower, image, text, weight)


def grad_kernel(mp_ref, tower_ref, core_ref, image_ref, text_ref, carried_ref, *refs):
    pieces = refs[:-5]
    worker_ref, mine_ref, other_ref, lift_ref, rest_ref = refs[-5:]
    half = pieces[0].shape[0]
    shard_rows, width = worker_ref.shape
    blocks = 2 * mine_ref.shape[0]
    row_block = shard_rows // blocks
    owners = len(pieces) // 2
    for n, piece in enumerate(pieces):
        lift_ref[owner_rows(mp_ref[0], tower_ref[0], n // 2, n % 2, owners, half)] = piece[...]
    wide = 256

    def fill(feats_ref):
        count = feats_ref.shape[0]
        for start in range(0, width, wide):
            part = slice(start, start + wide)
            grad = jnp.dot(
                feats_ref[...], lift_ref[:, part], preferred_element_type=jnp.float32
            )
            worker_ref[:count, part] = (1.0 - beta_one) * grad + carried_ref[:count, part]
        if count < shard_rows:
            worker_ref[count:] = carried_ref[count:]

    @pl.when(tower_ref[0] == 0)
    def _():
        fill(image_ref)

    @pl.when(tower_ref[0] != 0)
    def _():
        fill(text_ref)

    comp = worker_ref[...]
    row_abs = jnp.sum(jnp.abs(comp), axis=1, keepdims=True)
    row = lax.broadcasted_iota(jnp.int32, (shard_rows, 1), 0)
    scale = jnp.zeros((shard_rows, 1), jnp.float32)
    for b in range(blocks):
        inside = (row >= b * row_block) & (row < (b + 1) * row_block)
        total = jnp.sum(jnp.where(inside, row_abs, 0.0), axis=0, keepdims=True)
        scale = jnp.where(inside, total / (row_block * width), scale)
    scale = jnp.broadcast_to(scale, (shard_rows, 128)).astype(jnp.bfloat16).astype(jnp.float32)
    scale = scale[:, 0:1]
    ramp = jnp.clip(comp / (scale + epsilon), -1.0, 1.0).astype(jnp.bfloat16)
    restored = scale * ramp.astype(jnp.float32)
    worker_ref[...] = comp - restored
    tall = mine_ref.shape[1]
    rest_ref[:shard_rows] = restored
    rest_ref[shard_rows:] = jnp.zeros((rest_ref.shape[0] - shard_rows, width), jnp.float32)
    valid = lax.broadcasted_iota(jnp.int32, (tall, 1), 0) < row_block
    even = core_ref[0] == 0
    for b in range(blocks // 2):
        first = 2 * b * row_block
        one = jnp.where(valid, rest_ref[first : first + tall], 0.0)
        two = jnp.where(valid, rest_ref[first + row_block : first + row_block + tall], 0.0)
        mine_ref[b] = jnp.where(even, one, two).astype(jnp.bfloat16)
        other_ref[b] = jnp.where(even, two, one).astype(jnp.bfloat16)


def graded(mp, tower, core, image, text, carried, pieces, blocks):
    shard_rows, width = carried.shape
    rows = image.shape[1]
    sent = jax.ShapeDtypeStruct((blocks // 2, 16, width), jnp.bfloat16)
    return pl.pallas_call(
        grad_kernel,
        in_specs=[pl.BlockSpec(memory_space=pltpu.SMEM)] * 3
        + [pl.BlockSpec(memory_space=pltpu.VMEM)] * (3 + len(pieces)),
        out_specs=[pl.BlockSpec(memory_space=pltpu.VMEM)] * 3,
        out_shape=[jax.ShapeDtypeStruct(carried.shape, jnp.float32), sent, sent],
        scratch_shapes=[
            pltpu.VMEM((rows, width), jnp.bfloat16),
            pltpu.VMEM((shard_rows + 16, width), jnp.float32),
        ],
        compiler_params=pltpu.CompilerParams(vmem_limit_bytes=32 * 2**20),
        cost_estimate=pl.CostEstimate(
            flops=2 * rows * shard_rows * width,
            bytes_accessed=2 * rows * width + 12 * shard_rows * width,
            transcendentals=0,
        ),
    )(mp, tower, core, image, text, carried, *pieces)


def server_kernel(got_ref, error_ref, new_ref, reply_ref, rest_ref):
    row_block, width = error_ref.shape
    halves = got_ref.shape[0]
    total = got_ref[0].astype(jnp.float32)
    for b in range(1, halves):
        total = total + got_ref[b].astype(jnp.float32)
    rest_ref[...] = total
    average = rest_ref[:row_block] / (2 * halves) + error_ref[...]
    scale = jnp.sum(jnp.sum(jnp.abs(average), axis=1, keepdims=True), axis=0, keepdims=True)
    scale = jnp.broadcast_to(scale / (row_block * width), (16, width))
    scale = scale.astype(jnp.bfloat16).astype(jnp.float32)
    ramp = jnp.clip(average / (scale[:row_block] + epsilon), -1.0, 1.0).astype(jnp.bfloat16)
    ramp = ramp.astype(jnp.float32)
    new_ref[...] = average - scale[:row_block] * ramp
    rest_ref[...] = scale
    rest_ref[:row_block] = ramp
    reply = rest_ref[...].astype(jnp.bfloat16)
    for b in range(halves):
        reply_ref[b] = reply


def served(got, error):
    return pl.pallas_call(
        server_kernel,
        in_specs=[pl.BlockSpec(memory_space=pltpu.VMEM)] * 2,
        out_specs=[pl.BlockSpec(memory_space=pltpu.VMEM)] * 2,
        out_shape=[
            jax.ShapeDtypeStruct(error.shape, jnp.float32),
            jax.ShapeDtypeStruct(got.shape, jnp.bfloat16),
        ],
        scratch_shapes=[pltpu.VMEM(got.shape[1:], jnp.float32)],
        compiler_params=pltpu.CompilerParams(vmem_limit_bytes=16 * 2**20),
        cost_estimate=pl.CostEstimate(
            flops=got.size, bytes_accessed=4 * got.size, transcendentals=0
        ),
    )(got, error)


def update_kernel(core_ref, near_ref, far_ref, params_ref, rate_ref, weights_ref, moment_ref):
    halves = near_ref.shape[0]
    row_block = params_ref.shape[0] // (2 * halves)
    even = core_ref[0] == 0
    for b in range(halves):
        near = near_ref[b].astype(jnp.float32)
        far = far_ref[b].astype(jnp.float32)
        for c, block in enumerate((jnp.where(even, near, far), jnp.where(even, far, near))):
            first = (2 * b + c) * row_block
            rows = slice(first, first + row_block)
            moment_ref[rows] = block[:row_block] * block[row_block : row_block + 1]
    weights_ref[...] = params_ref[...] - rate_ref[...] * moment_ref[...]


def updated(core, near, far, params, rate):
    shape = jax.ShapeDtypeStruct(params.shape, jnp.float32)
    return pl.pallas_call(
        update_kernel,
        in_specs=[pl.BlockSpec(memory_space=pltpu.SMEM)]
        + [pl.BlockSpec(memory_space=pltpu.VMEM)] * 4,
        out_specs=[pl.BlockSpec(memory_space=pltpu.VMEM)] * 2,
        out_shape=[shape, shape],
        compiler_params=pltpu.CompilerParams(vmem_limit_bytes=32 * 2**20),
        cost_estimate=pl.CostEstimate(
            flops=3 * params.size, bytes_accessed=20 * params.size, transcendentals=0
        ),
    )(core, near, far, params, rate)


XY = ("tower", "xh", "y")
X2 = ("xh", "y")
DP = ("xh", "y", "core")


def shifted(block, axis, count, shift):
    return lax.ppermute(block, axis, [((i + shift) % count, i) for i in range(count)])


def crossed(block, axis, count, flip):
    return lax.ppermute(block, axis, [(i, i ^ flip) for i in range(count)])


def from_each(blocks, axis):
    return lax.all_to_all(blocks, axis, split_axis=0, concat_axis=0, tiled=True)


def ring_blocks(block, axis, count, ahead_count, direct=()):
    blocks = [block] * count
    for k in direct:
        blocks[k] = shifted(block, axis, count, k)
    ahead = behind = block
    for k in range(1, count):
        if k <= ahead_count and k not in direct:
            ahead = blocks[k] = shifted(ahead, axis, count, 1)
        if count - k > ahead_count and count - k not in direct:
            behind = blocks[count - k] = shifted(behind, axis, count, -1)
    return blocks


def ring_sum(term, axis, count, ahead_count, direct=()):
    wide, narrow = jnp.float32, jnp.bfloat16
    ahead_steps = [k for k in range(1, ahead_count + 1) if k not in direct]
    behind_steps = [k for k in range(ahead_count + 1, count) if k not in direct]
    total = term(0)
    for k in direct:
        total = total + shifted(term(k).astype(narrow), axis, count, -k).astype(wide)
    for steps, shift in ((ahead_steps[::-1], -1), (behind_steps, 1)):
        passed = None
        for k in steps:
            held = term(k) if passed is None else passed + term(k)
            passed = shifted(held.astype(narrow), axis, count, shift).astype(wide)
        total = total + passed
    return total


def body(
    image_feats,
    text_feats,
    labels,
    logit_scale,
    params,
    momentum,
    variance,
    worker_error,
    server_error,
):
    tower = lax.axis_index("tower")
    x_hi = lax.axis_index("xh")
    y = lax.axis_index("y")
    core = lax.axis_index("core")
    mp = lax.axis_index("mp")
    mp_count = lax.axis_size("mp")
    dp_count = lax.axis_size(DP)
    xy_count = lax.axis_size(XY)
    group_rows = image_feats.shape[0]
    per_dev = group_rows // mp_count
    half = per_dev // 2
    line = mp_count * half
    text_width = text_feats.shape[1]
    shard_rows = params.shape[2]
    width = params.shape[3]
    row_block = shard_rows // dp_count
    is_image = tower == 0
    f32, bf16 = jnp.float32, jnp.bfloat16

    mp_at, tower_at, core_at = (i.astype(jnp.int32).reshape(1) for i in (mp, tower, core))
    image, text = image_feats.T, text_feats.T
    partial = projected(mp_at, tower_at, image, text, params[0, 0], mp_count)

    def embedded(part):
        raw = ring_sum(
            lambda k: partial[2 * k + part].astype(f32), "mp", mp_count, mp_count // 2 - part
        )
        norm = jnp.sqrt(jnp.sum(raw * raw, axis=1, keepdims=True) + epsilon)
        unit = raw / norm
        return unit, norm, unit.astype(bf16)

    out_unit, out_norm, out_emb = embedded(0)
    swapped = crossed(out_emb, "tower", 2, 1)
    kept_unit, kept_norm, kept = embedded(1)
    image_own = jnp.where(is_image, kept, swapped)
    text_own = jnp.where(is_image, swapped, kept)

    cols = from_each(
        jnp.broadcast_to(text_own[None], (xy_count, half, width)), XY
    ).reshape(xy_count * half, width)
    near = joined(mp_at, ring_blocks(image_own, "mp", mp_count, 4, (4,)))
    far = crossed(near, "core", 2, 1)

    place = (x_hi * 4 + y) * 2
    label_blocks = labels.reshape(dp_count, mp_count, 2, half)

    def line_labels(which_core):
        one = lax.dynamic_index_in_dim(label_blocks, place + which_core, 0, False)
        return lax.dynamic_index_in_dim(one, tower, 1, False).reshape(1, -1)

    row_target = jnp.concatenate([line_labels(core), line_labels(1 - core)], 1).astype(f32)
    owner = jnp.arange(xy_count, dtype=jnp.int32)
    col_index = (
        ((owner % 8 * 2 + core) * group_rows + mp * per_dev + owner // 8 * half)[:, None]
        + jnp.arange(half, dtype=jnp.int32)[None, :]
    ).reshape(1, -1).astype(f32)
    row_target, col_index = lax.optimization_barrier((row_target, col_index))

    carried = beta_one * momentum[0, 0] + worker_error[0, 0, 0]
    rate = step_size / (jnp.sqrt(variance[0, 0]) + var_floor)
    cols, carried, rate = lax.optimization_barrier((cols, carried, rate))

    row_sums, col_sums = scored(core_at, logit_scale, near, far, cols, xy_count)

    col_sums = from_each(col_sums, XY)
    row_sums = lax.psum(row_sums + crossed(row_sums, "core", 2, 1), "mp")

    near_part, far_part, col_part = sloped(
        core_at, logit_scale, row_sums, row_target, col_sums, col_index, near, far, cols
    )

    passed = crossed(far_part, "core", 2, 1)
    text_grad = jnp.sum(
        from_each(col_part.reshape(xy_count, half, width), XY).astype(f32), axis=0
    )
    sent = parted(mp_at, near_part, passed, mp_count)
    image_grad = ring_sum(lambda k: sent[k].astype(f32), "mp", mp_count, 4, (4, 3, 5))

    kept_grad = jnp.where(is_image, image_grad, text_grad)
    out_grad = crossed(
        jnp.where(is_image, text_grad, image_grad).astype(bf16), "tower", 2, 1
    ).astype(f32)

    def lifted(unit, norm, grad):
        inner = jnp.sum(unit * grad, axis=1, keepdims=True)
        return ((grad - unit * inner) / norm).astype(bf16)

    kept_blocks = ring_blocks(lifted(kept_unit, kept_norm, kept_grad), "mp", mp_count, 3)
    out_blocks = ring_blocks(lifted(out_unit, out_norm, out_grad), "mp", mp_count, 4)
    worker_new, mine, other = graded(
        mp_at,
        tower_at,
        core_at,
        image,
        text,
        carried,
        [block for both in zip(out_blocks, kept_blocks) for block in both],
        dp_count,
    )

    pair = mine.astype(f32) + crossed(other, "core", 2, 1).astype(f32)
    server_new, reply = served(from_each(pair.astype(bf16), X2), server_error[0, 0])
    near_reply = from_each(reply, X2)
    far_reply = crossed(near_reply, "core", 2, 1)
    weights_new, momentum_new = updated(core_at, near_reply, far_reply, params[0, 0], rate)
    return (
        weights_new[None, None],
        momentum_new[None, None],
        worker_new[None, None, None],
        server_new[None, None],
    )


def solution(mesh):
    fine = Mesh(mesh.devices.reshape(2, 2, 4, 2, 8), ("tower", "xh", "y", "core", "mp"))
    return jax.shard_map(
        body,
        mesh=fine,
        in_specs=(
            P(DP, "mp"),
            P(DP, "mp"),
            P(),
            P(),
            P("tower", "mp", None, None),
            P("tower", "mp", None, None),
            P("tower", "mp", None, None),
            P("tower", DP, "mp", None, None),
            P("tower", "mp", DP, None),
        ),
        out_specs=(
            P("tower", "mp", None, None),
            P("tower", "mp", None, None),
            P("tower", DP, "mp", None, None),
            P("tower", "mp", DP, None),
        ),
        check_vma=False,
    )
```
